512 devices in a mesh: tile: 128 (over z, x, core), depth: 4 (over y).
Axes of the slice: x: 4, y: 4, z: 16, core: 2. Of those that a mesh axis runs over, the one named last changes fastest.
Arguments:
- substrate_start: float32 [4, 2, 16, 256, 1024], P(None, None, 'depth', 'tile'), may hold values from -6 to 6
- adatom_start: float32 [40, 2, 393216], P(None, None, ('tile', 'depth')), may hold values from -6 to 6
- disorder: float32 [16, 256, 1024], P('depth', 'tile'), may hold values from -0.4 to 0.4
- adatom_block: float32 [40, 40], replicated, as said below
- coupling: float32 [4, 40], replicated, may hold values from -1 to 1
- adatom_tile: int32 [393216, 1], P(('tile', 'depth')), may hold values from 0 to 127; in each aligned block of 768 rows (0 to 767, 768 to 1535, ...) at most 12 rows name the same one
- adatom_spot: int32 [393216], P(('tile', 'depth')), may hold values from 0 to 2047
Outputs:
- substrate_prev: float32 [4, 2, 16, 256, 1024], P(None, None, 'depth', 'tile')
- substrate_last: float32 [4, 2, 16, 256, 1024], P(None, None, 'depth', 'tile')
- adatom_prev: float32 [40, 2, 393216], P(None, None, ('tile', 'depth'))
- adatom_last: float32 [40, 2, 393216], P(None, None, ('tile', 'depth'))
The draws below stay inside these ranges and needn't reach their ends.
Inputs may be any that keep to these rules, and one draw needn't show every extreme that they name: `adatom_tile`: among the adatoms of one device, no tile is named by more than 12. adatom_block is symmetric.
All inputs are finite; a program needn't handle non-finite values.
Results may differ from the reference program's by a relative error of at most 0.0003.
Values sent between devices are 32-bit elements; how exact they have to be, the bound alone decides.
No kernel may reach another device: no remote copies, remote signals or barrier semaphores. Data moves between devices by JAX's collectives and lax.ppermute only.
A program may use at most 64 MiB of HBM per device.

```python
import math
import jax
import jax.numpy as jnp
import numpy as np
from jax import lax

ORB = 4
VECS = 2
CX = 2
NY = 1024
ORBA = 40
ADEV = 768
STEPS = 3
NL = 16
NX = 256
NAD = 393216
CAP = 12
N_TILE = 128


def draw_adatom_block(key, part):
    key = jax.random.fold_in(key, 7)
    raw = jax.random.normal(key, (ORBA, ORBA), jnp.float32)
    return ((raw + raw.T) * (0.5 / math.sqrt(ORBA))).astype(jnp.float32)


def with_ends(values, rng, low, top_value):
    extent = values.shape
    place = [jax.random.randint(jax.random.fold_in(rng, axis), (), 0, extent[axis]) for axis in range(len(extent))]
    values = values.at[tuple(place)].set(low)
    longest = extent.index(max(extent))
    place[longest] = (place[longest] + 1) % extent[longest]
    return values.at[tuple(place)].set(top_value)


def shard_levels(own_key, extent, shards, smallest, largest):
    def one(position, shards_of):
        draws = jax.random.uniform(jax.random.fold_in(jax.random.fold_in(own_key, 6), position), (shards_of,), jnp.float32, smallest / len(shards), largest / len(shards))
        return jnp.repeat(jnp.exp(draws), extent[position] // shards_of).reshape((-1,) + (1,) * (len(extent) - position - 1))

    gain = one(*shards[0])
    for cut in shards[1:]:
        gain = gain * one(*cut)
    return gain


def routed_block(rng, own, number, rows, amount, top, most, slope):
    order = jax.random.permutation(rng, amount)
    heavy_load, ordinary = load_shares(amount, rows * top, most, slope, True), load_shares(amount, rows * top, most, slope, False)
    places = jnp.arange(amount)

    def named(lengths, rotation):
        used = int((lengths > 0).sum())
        fixed = max(1, used // 4)
        shifted = fixed + (places - fixed + rotation * (used - fixed)) % max(1, amount - fixed)
        return jnp.zeros((amount,), jnp.int32).at[order[jnp.where(places < fixed, places, shifted)]].set(jnp.asarray(lengths, jnp.int32))

    lengths = jnp.where(number % 4 == 0, named(heavy_load, number // 4), named(ordinary, number - number // 4 - 1))
    mixed = jax.random.permutation(jax.random.fold_in(own, 3), amount)
    giver, receiver = mixed[0:amount // 2 * 2:2], mixed[1:amount // 2 * 2:2]
    room = jnp.minimum(lengths[giver] - 1, most - lengths[receiver]) // 2
    room = jnp.where((giver == order[0]) | (receiver == order[0]) | (lengths[receiver] == 0), 0, jnp.maximum(room, 0))
    shifted = jax.random.randint(jax.random.fold_in(own, 4), (amount // 2,), 0, 1 << 20) % (room + 1)
    lengths = lengths.at[giver].add(-shifted).at[receiver].add(shifted)
    labels = jnp.searchsorted(jnp.cumsum(lengths), jnp.arange(rows * top), side="right").astype(jnp.int32)
    grid = labels.reshape(top, rows).T
    grid = grid[jax.random.permutation(jax.random.fold_in(own, 1), rows)]
    rotation = jax.random.randint(jax.random.fold_in(own, 2), (rows, 1), 0, top)
    return jnp.take_along_axis(grid, (jnp.arange(top)[None, :] + rotation) % top, axis=1)


def load_shares(number_of, total, limit, slope, full):
    loads = [(1 << 20) // math.isqrt(grade ** slope) + 1 for grade in range(1, number_of + 1)]
    largest = limit if full else min(limit, max(-(-total // number_of), total * loads[0] // sum(loads)))
    least = 1 if total - largest >= number_of - 1 else 0
    given, spare = [largest] + [least] * (number_of - 1), total - largest - least * (number_of - 1)
    while spare > 0:
        candidates = [i for i in range(1, number_of) if given[i] < largest] or [i for i in range(1, number_of) if given[i] < limit]
        pool, budget = sum([loads[i] for i in candidates]), spare
        for i in candidates:
            addition = min(limit - given[i], max(1, budget * loads[i] // pool), spare)
            given[i] = given[i] + addition
            spare = spare - addition
    return np.array(given)


def normal_values(own_key, extent, deviation, bound, cuts=(), kind=jnp.bfloat16):
    entries = jax.random.normal(own_key, extent, jnp.float32) * deviation
    if len(cuts) > 0:
        entries = shard_levels(own_key, extent, cuts, -0.22, 0.18) * entries
    return jnp.clip(entries, min=-bound, max=bound).astype(kind)


def setup_inputs(seed: int = 0) -> dict:
    splits = jax.random.split(jax.random.key(seed), 8)
    substrate_start = normal_values(splits[0], (ORB, VECS, NL, NX, NY), 1.0, 6.0, ((2, 4), (3, 128)), jnp.float32)
    adatom_start = normal_values(splits[1], (ORBA, VECS, NAD), 1.0, 6.0, ((2, 512),), jnp.float32)
    disorder = jnp.clip(jax.random.uniform(splits[2], (NL, NX, NY), jnp.float32, -0.4, 0.4) * shard_levels(splits[2], (NL, NX, NY), ((0, 4), (1, 128)), -0.4, 0.0), -0.4, 0.4)
    adatom_block = draw_adatom_block(jax.random.fold_in(splits[7], 71), 0)
    coupling = normal_values(splits[4], (ORB, ORBA), ORBA ** -0.5, 1.0, (), jnp.float32)
    adatom_tile_keys = jax.random.split(jax.random.fold_in(splits[5], 1), NAD // ADEV)
    adatom_tile_turns = jax.random.permutation(jax.random.fold_in(splits[5], 3), NAD // ADEV)
    adatom_tile = jax.vmap(lambda own, number: routed_block(jax.random.fold_in(splits[5], 2), own, number, ADEV, N_TILE, 1, CAP, 2))(adatom_tile_keys, adatom_tile_turns).reshape((NAD, 1))
    adatom_spot = with_ends(jax.random.randint(splits[6], (NAD,), 0, CX * NY), jax.random.fold_in(splits[6], 1), 0, (CX * NY) - 1).astype(jnp.int32)
    return {"substrate_start": substrate_start, "adatom_start": adatom_start, "disorder": disorder, "adatom_block": adatom_block, "coupling": coupling, "adatom_tile": adatom_tile, "adatom_spot": adatom_spot}


hopping = 0.12
chemical = 0.15
pairing = 0.3


def substrate_terms(padded, field, disorder):
    beside = padded[:, :, 2:, 1:-1] + padded[:, :, :-2, 1:-1]
    beside = beside + padded[:, :, 1:-1, 2:] + padded[:, :, 1:-1, :-2]
    widened = jnp.pad(field, ((0, 0), (0, 0), (0, 0), (0, 0), (1, 1)))
    beside = beside + widened[..., 2:] + widened[..., :-2]
    signs = jnp.array([1.0, 1.0, -1.0, -1.0], jnp.float32).reshape(4, 1, 1, 1, 1)
    onsite = (disorder - chemical)[None, None] * field - hopping * beside
    partner = jnp.concatenate([field[2:], field[:2]], axis=0)
    return signs * onsite + pairing * partner


def operate(sub, adatoms, disorder, adatom_block, coupling, site):
    padded = jnp.pad(sub, ((0, 0), (0, 0), (1, 1), (1, 1), (0, 0)))
    sub_out = substrate_terms(padded, sub, disorder)
    orbs, vecs, layers, rows, cols = sub.shape
    surface = sub[:, :, 0].reshape(orbs * vecs, rows * cols)
    below = surface[:, site].reshape(orbs, vecs, -1)
    ad_out = jnp.einsum("ab,bvn->avn", adatom_block, adatoms, precision=lax.Precision.HIGHEST)
    ad_out = ad_out + jnp.einsum("oa,ovn->avn", coupling, below, precision=lax.Precision.HIGHEST)
    contrib = jnp.einsum("oa,avn->ovn", coupling, adatoms, precision=lax.Precision.HIGHEST)
    contrib = contrib.reshape(orbs * vecs, -1)
    added = jnp.zeros((orbs * vecs, rows * cols), jnp.float32).at[:, site].add(contrib)
    sub_out = sub_out.at[:, :, 0].add(added.reshape(orbs, vecs, rows, cols))
    return sub_out, ad_out


def reference(substrate_start, adatom_start, disorder, adatom_block, coupling, adatom_tile, adatom_spot):
    site = (adatom_tile[:, 0] * (CX * NY) + adatom_spot).astype(jnp.int32)
    prev_sub, prev_ad = substrate_start, adatom_start
    cur_sub, cur_ad = operate(prev_sub, prev_ad, disorder, adatom_block, coupling, site)
    for step in range(STEPS - 1):
        new_sub, new_ad = operate(cur_sub, cur_ad, disorder, adatom_block, coupling, site)
        new_sub = 2.0 * new_sub - prev_sub
        new_ad = 2.0 * new_ad - prev_ad
        prev_sub, prev_ad = cur_sub, cur_ad
        cur_sub, cur_ad = new_sub, new_ad
    return prev_sub, cur_sub, prev_ad, cur_ad
```

```python
import jax
import jax.numpy as jnp
from jax import lax
from jax.experimental import pallas as pl
from jax.experimental.pallas import tpu as pltpu
from jax.sharding import PartitionSpec as P

HOP = 0.12
MU = 0.15
PAIR = 0.3
CAP = 12
LANES = 32
EXACT = lax.Precision.HIGHEST
F32 = jnp.float32
BF16 = jnp.bfloat16


def iota(shape, dim):
    return lax.broadcasted_iota(jnp.int32, shape, dim)


def split(x):
    high = x.astype(BF16)
    return high, (x - high.astype(F32)).astype(BF16)


def dot(a, b):
    return jnp.dot(a, b, preferred_element_type=F32)


def dot3(a, b):
    return dot(a[0], b[0]) + dot(a[0], b[1]) + dot(a[1], b[0])


def dot_rows(a, b):
    return lax.dot_general(a, b, (((1,), (1,)), ((), ())), preferred_element_type=F32)


def beside(s):
    rank = s.ndim
    sub, lane = iota(s.shape, rank - 2), iota(s.shape, rank - 1)
    left = pltpu.roll(s, 1, rank - 1)
    left = jnp.where(lane == 0, pltpu.roll(left, 1, rank - 2), left)
    left = jnp.where((lane == 0) & (sub == 0), 0.0, left)
    right = pltpu.roll(s, 127, rank - 1)
    right = jnp.where(lane == 127, pltpu.roll(right, 7, rank - 2), right)
    right = jnp.where((lane == 127) & (sub == 7), 0.0, right)
    return left + right


def local_part(s, disorder, around):
    inner = (disorder - MU) * s - HOP * around
    return jnp.concatenate(
        [inner[:4] + PAIR * s[4:], PAIR * s[:4] - inner[4:]], axis=0
    )


def signed(s):
    return jnp.concatenate([s[:4], -s[4:]], axis=0)


def route_kernel(a_ref, tile_ref, spot_ref, block_ref, coup_ref, msg_ref, rank_ref):
    count = a_ref.shape[2]
    tiles = msg_ref.shape[0]
    a = split(jnp.concatenate([a_ref[0], a_ref[1]], axis=1))
    c, b = coup_ref[...], block_ref[...]
    cb = jnp.dot(c, b, precision=EXACT, preferred_element_type=F32)
    cbb = jnp.dot(cb, b, precision=EXACT, preferred_element_type=F32)
    w = jnp.concatenate([c, cb, cbb], axis=0)
    i, j = iota((24, 12), 0), iota((24, 12), 1)
    spread = (j == (i // 8) * 4 + (i % 8) // 2).astype(F32)
    w = split(jnp.dot(spread, w, precision=EXACT, preferred_element_type=F32))
    g = dot3(w, a)
    val = jnp.where(iota((24, count), 0) % 2 == 0, g[:, :count], g[:, count:])
    spot = spot_ref[...]
    row, col = spot >> 10, spot & 1023
    below = jnp.where(row == 0, col + 1025, 0)
    above = jnp.where(row == 1, col + 1, 0)
    vals = jnp.concatenate(
        [val, (spot + 1).astype(F32), below.astype(F32), above.astype(F32), jnp.zeros((5, count), F32)],
        axis=0,
    )
    hot = (iota((tiles, count), 0) == tile_ref[...]).astype(F32)
    hot16 = hot.astype(BF16)
    earlier = (iota((count, count), 0) < iota((count, count), 1)).astype(F32).astype(BF16)
    rank = jnp.sum(dot(hot16, earlier) * hot, axis=0, keepdims=True).astype(jnp.int32)
    rank_ref[...] = rank
    slots = split(
        jnp.concatenate([jnp.where(rank == r, vals, 0.0) for r in range(CAP)], axis=0)
    )
    msg = dot_rows(hot16, slots[0]) + dot_rows(hot16, slots[1])
    at, kind = iota(msg.shape, 0), iota(msg.shape, 1) % LANES
    up = jnp.where(at == tiles - 1, 0.0, pltpu.roll(msg, tiles - 1, 0))
    down = jnp.where(at == 0, 0.0, pltpu.roll(msg, 1, 0))
    msg_ref[:, 0, :] = jnp.where(kind == 25, up, jnp.where(kind == 26, down, msg))


def pure_kernel(pos_ref, x_ref, lo_ref, hi_ref, top_ref, one_ref, two_ref, s1_ref):
    first_layer = pos_ref[0] == 0
    last_layer = pos_ref[0] == pos_ref[1] - 1
    first_row = pos_ref[2] == 0
    last_row = pos_ref[2] == pos_ref[3] - 1

    def inside(l, r):
        out = None
        if l < 0:
            out = first_layer
        if l > 3:
            out = last_layer
        if r < 0:
            out = first_row if out is None else out | first_row
        if r > 1:
            out = last_row if out is None else out | last_row
        return out

    def masked(s, l, r):
        out = inside(l, r)
        return s if out is None else jnp.where(out, 0.0, s)

    def start(l, r):
        if r < 0:
            return lo_ref[:, l + 2, r + 2]
        if r > 1:
            return hi_ref[:, l + 2, r - 2]
        return x_ref[:, l + 3, r]

    def s0(l, r):
        return start(l, r)[:8]

    for l in range(-2, 6):
        for r in range(-1, 3):
            if r in (-1, 2) and l in (-2, 5):
                continue
            here = start(l, r)
            s = here[:8]
            around = beside(s) + s0(l - 1, r) + s0(l + 1, r) + s0(l, r - 1) + s0(l, r + 1)
            s1_ref[:, l + 2, r + 1] = masked(local_part(s, here[8:9], around), l, r)
    for l in range(-1, 5):
        for r in range(2):
            s = s1_ref[:, l + 2, r + 1]
            around = beside(s) + s1_ref[:, l + 1, r + 1] + s1_ref[:, l + 3, r + 1]
            around = around + s1_ref[:, l + 2, r] + s1_ref[:, l + 2, r + 2]
            new = 2.0 * local_part(s, x_ref[8:9, l + 3, r], around) - s0(l, r)
            two_ref[:, l + 1, r] = masked(new, l, r)
            if 0 <= l < 4:
                one_ref[:, l, r] = s
            if l == 0:
                rows = pl.ds(8 * r, 8)
                under = s1_ref[:, l + 3, r + 1]
                top_ref[0:8, rows, :] = s
                top_ref[8:16, rows, :] = -2.0 * HOP * signed(under) - s0(l, r)
                top_ref[16:25, rows, :] = start(l, r)
                top_ref[25:26, rows, :] = jnp.zeros((1, 8, 128), F32)


def columns(got):
    width = got.shape[1] // 128
    return jnp.concatenate([got[:, 128 * j : 128 * (j + 1)].T for j in range(width)], axis=0)


def scatter_kernel(pos_ref, got_ref, top_ref, out_ref, d2_ref, site_ref, dense_ref):
    got = got_ref[:, 0, :]
    tiles = got.shape[0]
    slots = columns(got)
    kind = iota((LANES, tiles), 0)
    lane = iota((tiles, 128), 1)
    for r in range(CAP):
        mine = slots[r * LANES : (r + 1) * LANES]
        sites = mine[24:27].astype(jnp.int32) - 1
        site_ref[r : r + 1] = sites[0:1]
        site_ref[16 + r : 17 + r] = sites[1:2]
        site_ref[32 + r : 33 + r] = sites[2:3]
        high = sites[0:1] >> 7
        vals = jnp.where(kind < 24, mine, jnp.where(kind == 24, 1.0, 0.0))
        near = vals.astype(BF16).astype(F32)
        rest = vals - near
        left = jnp.concatenate(
            [
                jnp.concatenate([jnp.where(high == h, part, 0.0) for h in range(16)], axis=0)
                for part in (near, rest)
            ],
            axis=1,
        ).astype(BF16)
        at = (got[:, r * LANES + 24 : r * LANES + 25].astype(jnp.int32) - 1) & 127
        right = (at == lane).astype(F32).astype(BF16)
        part = dot(left, jnp.concatenate([right, right], axis=0))
        dense_ref[...] = part if r == 0 else dense_ref[...] + part

    def dense(k):
        return dense_ref[pl.ds(k, 16, stride=LANES), :]

    on = pos_ref[0] == 0
    for k in range(8):
        q1 = dense(k) + jnp.where(on, top_ref[k], 0.0)
        q2 = 2.0 * dense(8 + k) + jnp.where(on, top_ref[8 + k], 0.0)
        d2 = dense(16 + k)
        d2_ref[k] = d2
        tail = jnp.where(on, top_ref[16 + k], d2)
        for y in range(4):
            out_ref[y, k] = q1
            out_ref[y, 8 + k] = q2
            out_ref[y, 16 + k] = tail
    number = dense(24)
    field = jnp.where(on, top_ref[24], 0.0)
    for y in range(4):
        out_ref[y, 24] = field
        out_ref[y, 25] = number


def evolve_kernel(
    pos_ref, m_ref, top_ref, d2_ref, site_ref, coup_ref, block_ref, two_ref,
    ans_ref, d_ref, low_ref, high_ref, f_ref, f1_ref,
):
    tiles = site_ref.shape[1]
    on = pos_ref[0] == 0
    c = coup_ref[...]
    cb = jnp.dot(c, block_ref[...], precision=EXACT, preferred_element_type=F32)
    nt = (((1,), (1,)), ((), ()))
    kk = lax.dot_general(c, c, nt, precision=EXACT, preferred_element_type=F32)
    kb = lax.dot_general(cb, c, nt, precision=EXACT, preferred_element_type=F32)

    def mix(k, s):
        def row(o):
            terms = [k[o : o + 1, q : q + 1] * s[2 * q : 2 * q + 2] for q in range(4)]
            return (terms[0] + terms[1]) + (terms[2] + terms[3])

        return jnp.concatenate([row(o) for o in range(4)], axis=0)

    def rows_of(s):
        return s.reshape(s.shape[0], 2, 8, 128)

    s0 = m_ref[0, 16:24]
    field = rows_of(m_ref[0, 24:25])
    s1 = (m_ref[0, 0:8] + m_ref[1, 0:8]) + (m_ref[2, 0:8] + m_ref[3, 0:8])
    q2 = (m_ref[0, 8:16] + m_ref[1, 8:16]) + (m_ref[2, 8:16] + m_ref[3, 8:16])
    number = (m_ref[0, 25:26] + m_ref[1, 25:26]) + (m_ref[2, 25:26] + m_ref[3, 25:26])

    def flat_part(s):
        s = rows_of(s)
        other = jnp.concatenate([s[:, 1:2], s[:, 0:1]], axis=1)
        return local_part(s, field, beside(s) + other).reshape(8, 16, 128)

    hopped = q2 + 2.0 * (number * mix(kk, s0))
    s2 = hopped + 2.0 * flat_part(s1)
    d0 = jnp.where(on, s1 - top_ref[0:8], 0.0)
    delta = jnp.where(on, hopped - top_ref[8:16] + 2.0 * flat_part(d0), 0.0)
    d2 = d2_ref[...] + (m_ref[1, 16:24] + m_ref[2, 16:24] + m_ref[3, 16:24])
    third = 2.0 * (d2 + number * (mix(kb, s0) + mix(kk, s1))) - d0
    d_ref[0:8] = d0
    d_ref[8:16] = delta
    d_ref[16:24] = jnp.where(on, third, 0.0)
    hop0 = -2.0 * HOP * signed(rows_of(d0))
    d0r, deltar = rows_of(d0), rows_of(delta)
    for r, ref in ((0, low_ref), (1, high_ref)):
        ref[:, 0] = two_ref[:, 1, r] + deltar[:, r]
        ref[:, 1] = two_ref[:, 2, r] + hop0[:, r]
        ref[:, 2] = two_ref[:, 3, r]
        ref[:, 3] = two_ref[:, 4, r]
        ref[:, 4] = d0r[:, r]

    for k in range(8):
        f_ref[pl.ds(k, 16, stride=24), :] = s0[k]
        f_ref[pl.ds(8 + k, 16, stride=24), :] = s1[k]
        f_ref[pl.ds(16 + k, 16, stride=24), :] = s2[k]
        f1_ref[pl.ds(k, 16, stride=8), :] = s1[k]
    f = jnp.concatenate(split(f_ref[...]), axis=1)
    f1 = jnp.concatenate(split(f1_ref[...]), axis=1)
    sub = iota((128, 2 * tiles), 0)

    def pick(table, width, sites):
        right = (sub == (sites & 127)).astype(F32).astype(BF16)
        found = dot(table, jnp.concatenate([right, right], axis=0))
        high = sites >> 7
        out = jnp.zeros((width, sites.shape[1]), F32)
        for h in range(16):
            out = out + jnp.where(high == h, found[h * width : (h + 1) * width], 0.0)
        return out

    own, low, high = [], [], []
    for r in range(0, CAP, 2):
        for table, width, base, out in ((f, 24, 0, own), (f1, 8, 16, low), (f1, 8, 32, high)):
            sites = jnp.concatenate(
                [site_ref[base + r : base + r + 1], site_ref[base + r + 1 : base + r + 2]], axis=1
            )
            both = pick(table, width, sites)
            out += [both[:, :tiles], both[:, tiles:]]
    answer = jnp.concatenate(own + low + high + [jnp.zeros((32, tiles), F32)], axis=0)
    for j in range(4):
        ans_ref[:, j, :] = answer[128 * j : 128 * (j + 1)].T


def adatom_kernel(a_ref, back_ref, tile_ref, rank_ref, block_ref, coup_ref, prev_ref, last_ref):
    count = a_ref.shape[2]
    tiles = back_ref.shape[0]
    back = jnp.concatenate([back_ref[:, j, :].T for j in range(4)], axis=0)
    back = jnp.concatenate(
        [back[:288], pltpu.roll(back[288:384], 1, 1), pltpu.roll(back[384:480], tiles - 1, 1)], axis=0
    )
    hot = (iota((tiles, count), 0) == tile_ref[...]).astype(F32).astype(BF16)
    found = dot(jnp.concatenate(split(back), axis=1), jnp.concatenate([hot, hot], axis=0))
    rank = rank_ref[...]
    s = jnp.zeros((24, count), F32)
    halo = jnp.zeros((8, count), F32)
    for r in range(CAP):
        here = rank == r
        s = s + jnp.where(here, found[24 * r : 24 * r + 24], 0.0)
        near = found[288 + 8 * r : 296 + 8 * r] + found[384 + 8 * r : 392 + 8 * r]
        halo = halo + jnp.where(here, near, 0.0)
    sign = jnp.where(iota((8, count), 0) < 4, 1.0, -1.0)
    s2 = s[16:24] - 2.0 * HOP * sign * halo
    b = split(block_ref[...])
    i, j = iota((4, 8), 0), iota((4, 8), 1)
    spread = (i == j // 2).astype(F32)
    c = split(
        lax.dot_general(
            coup_ref[...], spread, (((0,), (0,)), ((), ())), precision=EXACT, preferred_element_type=F32
        )
    )
    even = iota((8, count), 0) % 2 == 0

    def apply(a, s):
        s = jnp.concatenate([jnp.where(even, s, 0.0), jnp.where(even, 0.0, s)], axis=1)
        return dot3(b, split(a)) + dot3(c, split(s))

    a0 = jnp.concatenate([a_ref[0], a_ref[1]], axis=1)
    a1 = apply(a0, s[0:8])
    a2 = 2.0 * apply(a1, s[8:16]) - a0
    a3 = 2.0 * apply(a2, s2) - a1
    for v in range(2):
        prev_ref[v] = a2[:, v * count : (v + 1) * count]
        last_ref[v] = a3[:, v * count : (v + 1) * count]


def last_kernel(pos_ref, x_ref, one_ref, two_ref, d_ref, before_ref, after_ref, prev_ref, last_ref):
    has_before = pos_ref[2] > 0
    has_after = pos_ref[2] < pos_ref[3] - 1
    d0 = d_ref[0:8].reshape(8, 2, 8, 128)
    delta = d_ref[8:16].reshape(8, 2, 8, 128)
    third = d_ref[16:24].reshape(8, 2, 8, 128)

    def hop(s):
        return -2.0 * HOP * signed(s)

    hop0 = [hop(d0[:, r]) for r in range(2)]
    for r, ref in ((0, before_ref), (1, after_ref)):
        prev_ref[:, 0, r] = two_ref[:, 1, r] + delta[:, r] + hop(ref[:, 4])
        prev_ref[:, 1, r] = two_ref[:, 2, r] + hop0[r]
        prev_ref[:, 2, r] = two_ref[:, 3, r]
        prev_ref[:, 3, r] = two_ref[:, 4, r]

    def beyond(l, r):
        ref, there = (before_ref, has_before) if r == 0 else (after_ref, has_after)
        s = ref[:, l]
        if l == 0:
            s = s + jnp.where(there, hop0[r], 0.0)
        return s

    for l in range(4):
        for r in range(2):
            s = prev_ref[:, l, r]
            over = two_ref[:, 0, r] if l == 0 else prev_ref[:, l - 1, r]
            under = two_ref[:, 5, r] if l == 3 else prev_ref[:, l + 1, r]
            around = beside(s) + over + under + prev_ref[:, l, 1 - r] + beyond(l, r)
            new = 2.0 * local_part(s, x_ref[8:9, l + 3, r], around) - one_ref[:, l, r]
            if l == 0:
                new = new + 2.0 * third[:, r] - d0[:, r]
            last_ref[:, l, r] = new


VM = pl.BlockSpec(memory_space=pltpu.VMEM)
SM = pl.BlockSpec(memory_space=pltpu.SMEM)


def shape(*dims, dtype=F32):
    return jax.ShapeDtypeStruct(dims, dtype)


def call(kernel, name, outs, args, scratch=(), smem=False, cost=100_000):
    return pl.pallas_call(
        kernel,
        out_shape=outs,
        in_specs=[SM if smem and i == 0 else VM for i in range(len(args))],
        out_specs=[VM] * len(outs),
        scratch_shapes=list(scratch),
        name=name,
        cost_estimate=pl.CostEstimate(flops=cost, bytes_accessed=1_000_000, transcendentals=0),
        compiler_params=pltpu.CompilerParams(vmem_limit_bytes=40 * 2**20),
    )(*args)


def per_device(
    substrate_start, adatom_start, disorder, adatom_block, coupling, adatom_tile, adatom_spot
):
    tiles, depths = lax.axis_size("tile"), lax.axis_size("depth")
    t, y = lax.axis_index("tile"), lax.axis_index("depth")
    count = adatom_spot.shape[0]
    pos = jnp.stack([y, jnp.int32(depths), t, jnp.int32(tiles)])

    def shifted(x, axis, size, step):
        pairs = [(i, i + step) for i in range(size) if 0 <= i + step < size]
        return lax.ppermute(x, axis, pairs)

    x = jnp.concatenate(
        [substrate_start.reshape(8, 4, 2, 8, 128), disorder.reshape(1, 4, 2, 8, 128)], axis=0
    )
    above = shifted(x[:, 1:], "depth", depths, 1)
    below = shifted(x[:, :3], "depth", depths, -1)

    a = adatom_start.transpose(1, 0, 2)
    own_tile = adatom_tile.reshape(1, count)
    msg, rank = call(
        route_kernel, "route",
        (shape(tiles, 1, CAP * LANES), shape(1, count, dtype=jnp.int32)),
        (a, own_tile, adatom_spot.reshape(1, count), adatom_block, coupling),
    )
    got = lax.all_to_all(msg, "tile", split_axis=0, concat_axis=0, tiled=True)

    x = jnp.concatenate([above, x, below], axis=1)
    lo = shifted(x[:, 1:9], "tile", tiles, 1)
    hi = shifted(x[:, 1:9], "tile", tiles, -1)
    top, one, two = call(
        pure_kernel, "pure",
        (shape(26, 16, 128), shape(8, 4, 2, 8, 128), shape(8, 6, 2, 8, 128)),
        (pos, x, lo, hi),
        (pltpu.VMEM((8, 8, 4, 8, 128), F32),), smem=True,
    )
    part, d2, site = call(
        scatter_kernel, "scatter",
        (shape(4, 26, 16, 128), shape(8, 16, 128), shape(48, tiles, dtype=jnp.int32)),
        (pos, got, top),
        (pltpu.VMEM((16 * LANES, 128), F32),), smem=True,
    )
    part = lax.all_to_all(part, "depth", split_axis=0, concat_axis=0, tiled=True)
    answer, d, low, high = call(
        evolve_kernel, "evolve",
        (shape(tiles, 4, 128), shape(24, 16, 128), shape(8, 5, 8, 128), shape(8, 5, 8, 128)),
        (pos, part, top, d2, site, coupling, adatom_block, two),
        (pltpu.VMEM((384, 128), F32), pltpu.VMEM((128, 128), F32)), smem=True,
    )
    before = shifted(high, "tile", tiles, 1)
    after = shifted(low, "tile", tiles, -1)
    back = lax.all_to_all(answer, "tile", split_axis=0, concat_axis=0, tiled=True)
    sub_prev, sub_last = call(
        last_kernel, "last",
        (shape(8, 4, 2, 8, 128), shape(8, 4, 2, 8, 128)),
        (pos, x, one, two, d, before, after), smem=True,
    )
    ad_prev, ad_last = call(
        adatom_kernel, "adatoms",
        (shape(2, 40, count), shape(2, 40, count)),
        (a, back, own_tile, rank, adatom_block, coupling),
    )
    return (
        sub_prev.reshape(4, 2, 4, 2, 1024),
        sub_last.reshape(4, 2, 4, 2, 1024),
        ad_prev.transpose(1, 0, 2),
        ad_last.transpose(1, 0, 2),
    )


def solution(mesh):
    in_specs = (
        P(None, None, "depth", "tile", None),
        P(None, None, ("tile", "depth")),
        P("depth", "tile", None),
        P(),
        P(),
        P(("tile", "depth"), None),
        P(("tile", "depth")),
    )
    out_specs = (
        P(None, None, "depth", "tile", None),
        P(None, None, "depth", "tile", None),
        P(None, None, ("tile", "depth")),
        P(None, None, ("tile", "depth")),
    )
    return jax.shard_map(
        per_device, mesh=mesh, in_specs=in_specs, out_specs=out_specs, check_vma=False
    )
```

```python
import jax
import jax.numpy as jnp
from jax import lax
from jax.experimental import pallas as pl
from jax.experimental.pallas import tpu as pltpu
from jax.sharding import PartitionSpec as P

HOP = 0.12
MU = 0.15
PAIR = 0.3
CAP = 12
LANES = 32
EXACT = lax.Precision.HIGHEST
F32 = jnp.float32
BF16 = jnp.bfloat16


def iota(shape, dim):
    return lax.broadcasted_iota(jnp.int32, shape, dim)


def split(x):
    high = x.astype(BF16)
    return high, (x - high.astype(F32)).astype(BF16)


def dot(a, b):
    return jnp.dot(a, b, preferred_element_type=F32)


def dot3(a, b):
    return dot(a[0], b[0]) + dot(a[0], b[1]) + dot(a[1], b[0])


def dot_rows(a, b):
    return lax.dot_general(a, b, (((1,), (1,)), ((), ())), preferred_element_type=F32)


def beside(s):
    rank = s.ndim
    sub, lane = iota(s.shape, rank - 2), iota(s.shape, rank - 1)
    left = pltpu.roll(s, 1, rank - 1)
    left = jnp.where(lane == 0, pltpu.roll(left, 1, rank - 2), left)
    left = jnp.where((lane == 0) & (sub == 0), 0.0, left)
    right = pltpu.roll(s, 127, rank - 1)
    right = jnp.where(lane == 127, pltpu.roll(right, 7, rank - 2), right)
    right = jnp.where((lane == 127) & (sub == 7), 0.0, right)
    return left + right


def local_part(s, disorder, around):
    inner = (disorder - MU) * s - HOP * around
    return jnp.concatenate(
        [inner[:4] + PAIR * s[4:], PAIR * s[:4] - inner[4:]], axis=0
    )


def signed(s):
    return jnp.concatenate([s[:4], -s[4:]], axis=0)


def stacked(w):
    high, low = split(w)
    return jnp.concatenate([high, low, high], axis=1)


def stacked_right(x):
    high, low = split(x)
    return jnp.concatenate([high, high, low], axis=0)


def route_kernel(
    a_hbm, tile_hbm, spot_hbm, block_hbm, coup_hbm, msg_ref, rank_ref,
    a_ref, tile_ref, spot_ref, block_ref, coup_ref, sems,
):
    pairs = (
        (tile_hbm, tile_ref), (spot_hbm, spot_ref), (a_hbm, a_ref), (block_hbm, block_ref), (coup_hbm, coup_ref)
    )
    copies = [pltpu.make_async_copy(src, dst, sems.at[i]) for i, (src, dst) in enumerate(pairs)]
    for copy in copies:
        copy.start()
    count = a_ref.shape[2]
    tiles = msg_ref.shape[0]
    part = 256
    earlier = (iota((part, part), 0) < iota((part, part), 1)).astype(F32).astype(BF16)
    copies[0].wait()
    hot = (iota((tiles, count), 0) == tile_ref[...]).astype(F32)
    hot16 = hot.astype(BF16)
    ranks, seen = [], jnp.zeros((tiles, 1), F32)
    for k in range(0, count, part):
        chunk = hot[:, k : k + part]
        ranks.append(jnp.sum((dot(hot16[:, k : k + part], earlier) + seen) * chunk, axis=0, keepdims=True))
        seen = seen + jnp.sum(chunk, axis=1, keepdims=True)
    rank = jnp.concatenate(ranks, axis=1).astype(jnp.int32)
    rank_ref[...] = rank
    for copy in copies[1:]:
        copy.wait()
    a = jnp.concatenate([a_ref[:, 0, :], a_ref[:, 1, :]], axis=1)
    c, b = coup_ref[...], block_ref[...]
    cb = jnp.dot(c, b, precision=EXACT, preferred_element_type=F32)
    cbb = jnp.dot(cb, b, precision=EXACT, preferred_element_type=F32)
    pad = jnp.zeros((12, 8), F32)
    w = jnp.concatenate([jnp.concatenate([c, cb, cbb], axis=0), pad], axis=1)
    a = jnp.concatenate([a, jnp.zeros((8, 2 * count), F32)], axis=0)
    g = dot(stacked(w), stacked_right(a))
    val = jnp.concatenate(
        [g[4 * k : 4 * k + 4, v * count : (v + 1) * count] for k in range(3) for v in range(2)], axis=0
    )
    spot = spot_ref[...].reshape(1, count)
    row, col = spot >> 10, spot & 1023
    below = jnp.where(row == 0, col + 1025, 0)
    above = jnp.where(row == 1, col + 1, 0)
    vals = jnp.concatenate(
        [val, (spot + 1).astype(F32), below.astype(F32), above.astype(F32), jnp.zeros((5, count), F32)],
        axis=0,
    )
    slots = split(
        jnp.concatenate([jnp.where(rank == r, vals, 0.0) for r in range(CAP)], axis=0)
    )
    msg = dot_rows(hot16, slots[0]) + dot_rows(hot16, slots[1])
    at, kind = iota(msg.shape, 0), iota(msg.shape, 1) % LANES
    up = jnp.where(at == tiles - 1, 0.0, pltpu.roll(msg, tiles - 1, 0))
    down = jnp.where(at == 0, 0.0, pltpu.roll(msg, 1, 0))
    msg_ref[:, 0, :] = jnp.where(kind == 25, up, jnp.where(kind == 26, down, msg))


CORNER = [(1, 1), (1, 2), (2, 1)]


def pack_kernel(lo_ref, hi_ref, above_ref, below_ref, after_ref, up_ref, down_ref):
    for i, (k, d) in enumerate(CORNER):
        for j, (ref, l) in enumerate(((above_ref, 3 - k), (below_ref, k - 1))):
            up_ref[:, 3 * j + i] = ref[:, l, 2 - d]
            down_ref[:, 3 * j + i] = ref[:, l, d - 1]
    for l in range(4):
        up_ref[:, 6 + l] = lo_ref[:, l, 1]
        down_ref[:, 6 + l] = hi_ref[:, l, 0]


def top_kernel(x_ref, lo_ref, hi_ref, coup_ref, block_ref, top_ref, mix_ref):
    c = coup_ref[...]
    cb = jnp.dot(c, block_ref[...], precision=EXACT, preferred_element_type=F32)
    nt = (((1,), (1,)), ((), ()))
    mix_ref[0] = lax.dot_general(c, c, nt, precision=EXACT, preferred_element_type=F32)
    mix_ref[1] = lax.dot_general(cb, c, nt, precision=EXACT, preferred_element_type=F32)

    def s0(l, r):
        return (lo_ref[:, l, r + 2] if r < 0 else hi_ref[:, l, r - 2] if r > 1 else x_ref[:, l, r])

    for r in range(2):
        rows = pl.ds(8 * r, 8)
        first = []
        for l in range(2):
            here = s0(l, r)
            s = here[:8]
            around = beside(s) + s0(l + 1, r)[:8] + s0(l, r - 1)[:8] + s0(l, r + 1)[:8]
            if l > 0:
                around = around + s0(l - 1, r)[:8]
            first.append(local_part(s, here[8:9], around))
        top_ref[0:8, rows, :] = first[0]
        top_ref[8:16, rows, :] = -2.0 * HOP * signed(first[1]) - s0(0, r)[:8]
        top_ref[16:25, rows, :] = s0(0, r)
        top_ref[25:26, rows, :] = jnp.zeros((1, 8, 128), F32)


def pure_kernel(
    pos_ref, x_ref, lo_ref, hi_ref, low2_ref, high2_ref, above_ref, below_ref, after_ref,
    one_ref, two_ref, s1_ref,
):
    first_layer = pos_ref[0] == 0
    last_layer = pos_ref[0] == pos_ref[1] - 1
    first_row = pos_ref[2] == 0
    last_row = pos_ref[2] == pos_ref[3] - 1

    def masked(s, l, r):
        out = None
        for cond, flag in (
            (l < 0, first_layer), (l > 3, last_layer), (r < 0, first_row), (r > 1, last_row)
        ):
            if cond:
                out = flag if out is None else out | flag
        return s if out is None else jnp.where(out, 0.0, s)

    def start(l, r):
        k, d = max(-l, l - 3), max(-r, r - 1)
        side = low2_ref if r < 0 else high2_ref
        if k > 0 and d > 0:
            return side[:, (0 if l < 0 else 3) + CORNER.index((k, d))]
        if k > 0:
            return above_ref[:, 3 - k, r] if l < 0 else below_ref[:, k - 1, r]
        if d > 2:
            return side[:, 6 + l]
        return (lo_ref[:, l, r + 2] if r < 0 else hi_ref[:, l, r - 2] if r > 1 else x_ref[:, l, r])

    def s0(l, r):
        return start(l, r)[:8]

    def beyond(l, r):
        return max(-l, l - 3, 0) + max(-r, r - 1, 0)

    for l in range(-2, 6):
        for r in range(-2, 4):
            if beyond(l, r) > 2:
                continue
            here = start(l, r)
            s = here[:8]
            around = beside(s) + s0(l - 1, r) + s0(l + 1, r) + s0(l, r - 1) + s0(l, r + 1)
            s1_ref[:, l + 2, r + 2] = masked(local_part(s, here[8:9], around), l, r)
    for l in range(-1, 5):
        for r in range(-1, 3):
            if beyond(l, r) > 1:
                continue
            s = s1_ref[:, l + 2, r + 2]
            around = beside(s) + s1_ref[:, l + 1, r + 2] + s1_ref[:, l + 3, r + 2]
            around = around + s1_ref[:, l + 2, r + 1] + s1_ref[:, l + 2, r + 3]
            new = 2.0 * local_part(s, start(l, r)[8:9], around) - s0(l, r)
            two_ref[:, l + 1, r + 1] = masked(new, l, r)
            if beyond(l, r) == 0:
                one_ref[:, l, r] = s


def columns(got):
    width = got.shape[1] // 128
    return jnp.concatenate([got[:, 128 * j : 128 * (j + 1)].T for j in range(width)], axis=0)


def scatter_kernel(pos_ref, got_ref, top_ref, out_ref, d2_ref, site_ref, dense_ref):
    got = got_ref[:, 0, :]
    tiles = got.shape[0]
    slots = columns(got)
    sub = iota((256, tiles), 0)
    total = None
    for r in range(CAP):
        vals = slots[r * LANES : r * LANES + 24]
        sites = slots[r * LANES + 24 : r * LANES + 27].astype(jnp.int32) - 1
        site_ref[r : r + 1] = sites[0:1]
        site_ref[16 + r : 17 + r] = sites[1:2]
        site_ref[32 + r : 33 + r] = sites[2:3]
        high = sites[0:1] >> 8
        near = vals.astype(BF16).astype(F32)
        number = (iota((8, tiles), 0) == high).astype(F32)
        left = jnp.concatenate(
            [
                jnp.concatenate([jnp.where(high == h, part, 0.0) for h in range(8)] + [last], axis=0)
                for part, last in ((near, number), (vals - near, jnp.zeros_like(number)))
            ],
            axis=1,
        ).astype(BF16)
        right = (sub == (sites[0:1] & 255)).astype(F32).astype(BF16)
        part = dot_rows(left, jnp.concatenate([right, right], axis=1))
        total = part if total is None else total + part
    dense_ref[0] = total[:, :128]
    dense_ref[1] = total[:, 128:]

    on = pos_ref[0] == 0
    for j in range(2):
        rows = pl.ds(j, 8, stride=2)

        def dense(k):
            k = k - k % 8 + (k % 2) * 4 + (k % 8) // 2
            return dense_ref[j, pl.ds(k, 8, stride=24), :]

        for k in range(8):
            q1 = dense(k) + jnp.where(on, top_ref[k, rows, :], 0.0)
            q2 = 2.0 * dense(8 + k) + jnp.where(on, top_ref[8 + k, rows, :], 0.0)
            d2 = dense(16 + k)
            d2_ref[k, rows, :] = d2
            tail = jnp.where(on, top_ref[16 + k, rows, :], d2)
            for y in range(4):
                out_ref[y, k, rows, :] = q1
                out_ref[y, 8 + k, rows, :] = q2
                out_ref[y, 16 + k, rows, :] = tail
        field = jnp.where(on, top_ref[24, rows, :], 0.0)
        for y in range(4):
            out_ref[y, 24, rows, :] = field
            out_ref[y, 25, rows, :] = dense_ref[j, 192:200, :]


def evolve_kernel(
    pos_ref, m_ref, top_ref, d2_ref, site_ref, mix_ref,
    ans_ref, d_ref, f_ref, f1_ref,
):
    tiles = site_ref.shape[1]
    on = pos_ref[0] == 0
    kk, kb = mix_ref[0], mix_ref[1]

    def mix(k, s):
        def row(o):
            terms = [k[o : o + 1, q : q + 1] * s[2 * q : 2 * q + 2] for q in range(4)]
            return (terms[0] + terms[1]) + (terms[2] + terms[3])

        return jnp.concatenate([row(o) for o in range(4)], axis=0)

    def rows_of(s):
        return s.reshape(s.shape[0], 2, 8, 128)

    s0 = m_ref[0, 16:24]
    field = rows_of(m_ref[0, 24:25])
    s1 = (m_ref[0, 0:8] + m_ref[1, 0:8]) + (m_ref[2, 0:8] + m_ref[3, 0:8])
    q2 = (m_ref[0, 8:16] + m_ref[1, 8:16]) + (m_ref[2, 8:16] + m_ref[3, 8:16])
    number = (m_ref[0, 25:26] + m_ref[1, 25:26]) + (m_ref[2, 25:26] + m_ref[3, 25:26])

    def flat_part(s):
        s = rows_of(s)
        other = jnp.concatenate([s[:, 1:2], s[:, 0:1]], axis=1)
        return local_part(s, field, beside(s) + other).reshape(8, 16, 128)

    hopped = q2 + 2.0 * (number * mix(kk, s0))
    s2 = hopped + 2.0 * flat_part(s1)
    d0 = jnp.where(on, s1 - top_ref[0:8], 0.0)
    delta = jnp.where(on, hopped - top_ref[8:16] + 2.0 * flat_part(d0), 0.0)
    d2 = d2_ref[...] + (m_ref[1, 16:24] + m_ref[2, 16:24] + m_ref[3, 16:24])
    third = 2.0 * (d2 + number * (mix(kb, s0) + mix(kk, s1))) - d0
    d_ref[0:8] = d0
    d_ref[8:16] = delta
    d_ref[16:24] = jnp.where(on, third, 0.0)
    for k in range(8):
        f_ref[pl.ds(k, 16, stride=24), :] = s0[k]
        f_ref[pl.ds(8 + k, 16, stride=24), :] = s1[k]
        f_ref[pl.ds(16 + k, 16, stride=24), :] = s2[k]
        f1_ref[pl.ds(k, 16, stride=8), :] = s1[k]
    f = jnp.concatenate(split(f_ref[...]), axis=1)
    f1 = jnp.concatenate(split(f1_ref[...]), axis=1)
    sub = iota((128, 2 * tiles), 0)

    def pick(table, width, sites):
        right = (sub == (sites & 127)).astype(F32).astype(BF16)
        found = dot(table, jnp.concatenate([right, right], axis=0))
        high = sites >> 7
        out = jnp.zeros((width, sites.shape[1]), F32)
        for h in range(16):
            out = out + jnp.where(high == h, found[h * width : (h + 1) * width], 0.0)
        return out

    own, low, high = [], [], []
    for r in range(0, CAP, 2):
        for table, width, base, out in ((f, 24, 0, own), (f1, 8, 16, low), (f1, 8, 32, high)):
            sites = jnp.concatenate(
                [site_ref[base + r : base + r + 1], site_ref[base + r + 1 : base + r + 2]], axis=1
            )
            both = pick(table, width, sites)
            out += [both[:, :tiles], both[:, tiles:]]
    answer = jnp.concatenate(own + low + high + [jnp.zeros((32, tiles), F32)], axis=0)
    for j in range(4):
        ans_ref[:, j, :] = answer[128 * j : 128 * (j + 1)].T


def adatom_kernel(a_ref, back_ref, tile_ref, rank_ref, block_ref, coup_ref, prev_ref, last_ref):
    count = a_ref.shape[2]
    tiles = back_ref.shape[0]
    back = jnp.concatenate([back_ref[:, j, :].T for j in range(4)], axis=0)
    back = jnp.concatenate(
        [back[:288], pltpu.roll(back[288:384], 1, 1), pltpu.roll(back[384:480], tiles - 1, 1)], axis=0
    )
    hot = (iota((tiles, count), 0) == tile_ref[...]).astype(F32).astype(BF16)
    found = dot(jnp.concatenate(split(back), axis=1), jnp.concatenate([hot, hot], axis=0))
    rank = rank_ref[...]
    s = jnp.zeros((24, count), F32)
    halo = jnp.zeros((8, count), F32)
    for r in range(CAP):
        here = rank == r
        s = s + jnp.where(here, found[24 * r : 24 * r + 24], 0.0)
        near = found[288 + 8 * r : 296 + 8 * r] + found[384 + 8 * r : 392 + 8 * r]
        halo = halo + jnp.where(here, near, 0.0)
    sign = jnp.where(iota((8, count), 0) < 4, 1.0, -1.0)
    s2 = s[16:24] - 2.0 * HOP * sign * halo
    i, j = iota((4, 8), 0), iota((4, 8), 1)
    spread = (i == j // 2).astype(F32)
    c = lax.dot_general(
        coup_ref[...], spread, (((0,), (0,)), ((), ())), precision=EXACT, preferred_element_type=F32
    )
    w = stacked(jnp.concatenate([block_ref[...], c], axis=1))
    even = iota((8, count), 0) % 2 == 0

    def apply(a, s):
        s = jnp.concatenate([jnp.where(even, s, 0.0), jnp.where(even, 0.0, s)], axis=1)
        return dot(w, stacked_right(jnp.concatenate([a, s], axis=0)))

    a0 = jnp.concatenate([a_ref[:, 0, :], a_ref[:, 1, :]], axis=1)
    a1 = apply(a0, s[0:8])
    a2 = 2.0 * apply(a1, s[8:16]) - a0
    a3 = 2.0 * apply(a2, s2) - a1
    for v in range(2):
        prev_ref[:, v, :] = a2[:, v * count : (v + 1) * count]
        last_ref[:, v, :] = a3[:, v * count : (v + 1) * count]


def last_kernel(pos_ref, x_ref, one_ref, two_ref, d_ref, before_ref, after_ref, prev_ref, last_ref):
    has_before = pos_ref[2] > 0
    has_after = pos_ref[2] < pos_ref[3] - 1
    d0 = d_ref[0:8].reshape(8, 2, 8, 128)
    delta = d_ref[8:16].reshape(8, 2, 8, 128)
    third = d_ref[16:24].reshape(8, 2, 8, 128)

    def hop(s):
        return -2.0 * HOP * signed(s)

    hop0 = [hop(d0[:, r]) for r in range(2)]
    for r, ref in ((0, before_ref), (1, after_ref)):
        prev_ref[:, 0, r] = two_ref[:, 1, r + 1] + delta[:, r] + hop(ref[0:8])
        prev_ref[:, 1, r] = two_ref[:, 2, r + 1] + hop0[r]
        prev_ref[:, 2, r] = two_ref[:, 3, r + 1]
        prev_ref[:, 3, r] = two_ref[:, 4, r + 1]

    def beyond(l, r):
        ref, there = (before_ref, has_before) if r == 0 else (after_ref, has_after)
        s = two_ref[:, l + 1, 3 * r]
        if l == 0:
            s = s + ref[8:16] + jnp.where(there, hop0[r], 0.0)
        if l == 1:
            s = s + hop(ref[0:8])
        return s

    for l in range(4):
        for r in range(2):
            s = prev_ref[:, l, r]
            over = two_ref[:, 0, r + 1] if l == 0 else prev_ref[:, l - 1, r]
            under = two_ref[:, 5, r + 1] if l == 3 else prev_ref[:, l + 1, r]
            around = beside(s) + over + under + prev_ref[:, l, 1 - r] + beyond(l, r)
            new = 2.0 * local_part(s, x_ref[8:9, l, r], around) - one_ref[:, l, r]
            if l == 0:
                new = new + 2.0 * third[:, r] - d0[:, r]
            last_ref[:, l, r] = new


VM = pl.BlockSpec(memory_space=pltpu.VMEM)
SM = pl.BlockSpec(memory_space=pltpu.SMEM)


def shape(*dims, dtype=F32):
    return jax.ShapeDtypeStruct(dims, dtype)


def call(kernel, name, outs, args, scratch=(), smem=False, cost=0, space=pltpu.VMEM, limit=16):
    return pl.pallas_call(
        kernel,
        out_shape=outs,
        in_specs=[SM if smem and i == 0 else pl.BlockSpec(memory_space=space) for i in range(len(args))],
        out_specs=[VM] * len(outs),
        scratch_shapes=list(scratch),
        name=name,
        cost_estimate=pl.CostEstimate(flops=cost, bytes_accessed=0, transcendentals=0),
        compiler_params=pltpu.CompilerParams(vmem_limit_bytes=limit * 2**20),
    )(*args)


def per_device(
    substrate_start, adatom_start, disorder, adatom_block, coupling, adatom_tile, adatom_spot
):
    tiles, depths = lax.axis_size("tile"), lax.axis_size("depth")
    t, y = lax.axis_index("tile"), lax.axis_index("depth")
    count = adatom_spot.shape[0]
    pos = jnp.stack([y, jnp.int32(depths), t, jnp.int32(tiles)])

    def shifted(x, axis, size, step):
        pairs = [(i, i + step) for i in range(size) if 0 <= i + step < size]
        return lax.ppermute(x, axis, pairs)

    own_tile = adatom_tile.reshape(1, count)
    msg, rank = call(
        route_kernel, "route",
        (shape(tiles, 1, CAP * LANES), shape(1, count, dtype=jnp.int32)),
        (adatom_start, own_tile, adatom_spot, adatom_block, coupling),
        (
            pltpu.VMEM((40, 2, count), F32), pltpu.VMEM((1, count), jnp.int32), pltpu.VMEM((count,), jnp.int32),
            pltpu.VMEM((40, 40), F32), pltpu.VMEM((4, 40), F32), pltpu.SemaphoreType.DMA((5,)),
        ),
        space=pl.ANY, limit=60
    )
    substrate, disorder, rank = lax.optimization_barrier((substrate_start, disorder, rank))
    got = lax.all_to_all(msg, "tile", split_axis=0, concat_axis=0, tiled=True)
    x = jnp.concatenate(
        [substrate.reshape(8, 4, 2, 8, 128), disorder.reshape(1, 4, 2, 8, 128)], axis=0
    )
    lo = shifted(x, "tile", tiles, 1)
    hi = shifted(x, "tile", tiles, -1)
    above = shifted(x[:, 1:], "depth", depths, 1)
    below = shifted(x[:, :3], "depth", depths, -1)
    top, mix = call(
        top_kernel, "top", (shape(26, 16, 128), shape(2, 4, 4)), (x, lo, hi, coupling, adatom_block)
    )
    part, d2, site = call(
        scatter_kernel, "scatter",
        (shape(4, 26, 16, 128), shape(8, 16, 128), shape(48, tiles, dtype=jnp.int32)),
        (pos, got, top),
        (pltpu.VMEM((2, 200, 128), F32),), smem=True,
    )
    above, below, part = lax.optimization_barrier((above, below, part))
    up, down = call(
        pack_kernel, "pack", (shape(9, 10, 8, 128), shape(9, 10, 8, 128)), (lo, hi, above, below, site)
    )
    low2 = shifted(up, "tile", tiles, 1)
    high2 = shifted(down, "tile", tiles, -1)
    part = lax.all_to_all(part, "depth", split_axis=0, concat_axis=0, tiled=True)
    answer, d = call(
        evolve_kernel, "evolve",
        (shape(tiles, 4, 128), shape(24, 16, 128)),
        (pos, part, top, d2, site, mix),
        (pltpu.VMEM((384, 128), F32), pltpu.VMEM((128, 128), F32)), smem=True,
    )
    before = shifted(d[:16, 8:], "tile", tiles, 1)
    after = shifted(d[:16, :8], "tile", tiles, -1)
    one, two = call(
        pure_kernel, "pure",
        (shape(8, 4, 2, 8, 128), shape(8, 6, 4, 8, 128)),
        (pos, x, lo, hi, low2, high2, above, below, d),
        (pltpu.VMEM((8, 8, 6, 8, 128), F32),), smem=True, cost=10**10,
    )
    back = lax.all_to_all(answer, "tile", split_axis=0, concat_axis=0, tiled=True)
    sub_prev, sub_last = call(
        last_kernel, "last",
        (shape(8, 4, 2, 8, 128), shape(8, 4, 2, 8, 128)),
        (pos, x, one, two, d, before, after), smem=True,
    )
    ad_prev, ad_last = call(
        adatom_kernel, "adatoms",
        (shape(40, 2, count), shape(40, 2, count)),
        (adatom_start, back, own_tile, rank, adatom_block, coupling),
    )
    return (
        sub_prev.reshape(4, 2, 4, 2, 1024),
        sub_last.reshape(4, 2, 4, 2, 1024),
        ad_prev,
        ad_last,
    )


def solution(mesh):
    in_specs = (
        P(None, None, "depth", "tile", None),
        P(None, None, ("tile", "depth")),
        P("depth", "tile", None),
        P(),
        P(),
        P(("tile", "depth"), None),
        P(("tile", "depth")),
    )
    out_specs = (
        P(None, None, "depth", "tile", None),
        P(None, None, "depth", "tile", None),
        P(None, None, ("tile", "depth")),
        P(None, None, ("tile", "depth")),
    )
    return jax.shard_map(
        per_device, mesh=mesh, in_specs=in_specs, out_specs=out_specs, check_vma=False
    )
```

```python
import jax
import jax.numpy as jnp
from jax import lax
from jax.experimental import pallas as pl
from jax.experimental.pallas import tpu as pltpu
from jax.sharding import PartitionSpec as P

HOP = 0.12
MU = 0.15
PAIR = 0.3
CAP = 12
LANES = 32
EXACT = lax.Precision.HIGHEST
F32 = jnp.float32
BF16 = jnp.bfloat16


def iota(shape, dim):
    return lax.broadcasted_iota(jnp.int32, shape, dim)


def split(x):
    high = x.astype(BF16)
    return high, (x - high.astype(F32)).astype(BF16)


def dot(a, b):
    return jnp.dot(a, b, preferred_element_type=F32)


def dot3(a, b):
    return dot(a[0], b[0]) + dot(a[0], b[1]) + dot(a[1], b[0])


def dot_rows(a, b):
    return lax.dot_general(a, b, (((1,), (1,)), ((), ())), preferred_element_type=F32)


def beside(s):
    rank = s.ndim
    sub, lane = iota(s.shape, rank - 2), iota(s.shape, rank - 1)
    left = pltpu.roll(s, 1, rank - 1)
    left = jnp.where(lane == 0, pltpu.roll(left, 1, rank - 2), left)
    left = jnp.where((lane == 0) & (sub == 0), 0.0, left)
    right = pltpu.roll(s, 127, rank - 1)
    right = jnp.where(lane == 127, pltpu.roll(right, 7, rank - 2), right)
    right = jnp.where((lane == 127) & (sub == 7), 0.0, right)
    return left + right


def local_part(s, disorder, around):
    inner = (disorder - MU) * s - HOP * around
    return jnp.concatenate(
        [inner[:4] + PAIR * s[4:], PAIR * s[:4] - inner[4:]], axis=0
    )


def signed(s):
    return jnp.concatenate([s[:4], -s[4:]], axis=0)


def stacked(w):
    high, low = split(w)
    return jnp.concatenate([high, low, high], axis=1)


def stacked_right(x):
    high, low = split(x)
    return jnp.concatenate([high, high, low], axis=0)


def route_kernel(
    a_hbm, tile_hbm, spot_hbm, block_hbm, coup_hbm, msg_ref, rank_ref,
    a_ref, tile_ref, spot_ref, block_ref, coup_ref, sems,
):
    pairs = (
        (tile_hbm, tile_ref), (spot_hbm, spot_ref), (block_hbm, block_ref), (coup_hbm, coup_ref), (a_hbm, a_ref)
    )
    copies = [pltpu.make_async_copy(src, dst, sems.at[i]) for i, (src, dst) in enumerate(pairs)]
    for copy in copies:
        copy.start()
    count = a_ref.shape[2]
    tiles = msg_ref.shape[0]
    part = 256
    earlier = (iota((part, part), 0) < iota((part, part), 1)).astype(F32).astype(BF16)
    for copy in copies[:4]:
        copy.wait()
    c, b = coup_ref[...], block_ref[...]
    cb = jnp.dot(c, b, precision=EXACT, preferred_element_type=F32)
    cbb = jnp.dot(cb, b, precision=EXACT, preferred_element_type=F32)
    hot = (iota((tiles, count), 0) == tile_ref[...]).astype(F32)
    hot16 = hot.astype(BF16)
    ranks, seen = [], jnp.zeros((tiles, 1), F32)
    for k in range(0, count, part):
        chunk = hot[:, k : k + part]
        ranks.append(jnp.sum((dot(hot16[:, k : k + part], earlier) + seen) * chunk, axis=0, keepdims=True))
        seen = seen + jnp.sum(chunk, axis=1, keepdims=True)
    rank = jnp.concatenate(ranks, axis=1).astype(jnp.int32)
    rank_ref[...] = rank
    copies[4].wait()
    a = jnp.concatenate([a_ref[:, 0, :], a_ref[:, 1, :]], axis=1)
    pad = jnp.zeros((12, 8), F32)
    w = jnp.concatenate([jnp.concatenate([c, cb, cbb], axis=0), pad], axis=1)
    a = jnp.concatenate([a, jnp.zeros((8, 2 * count), F32)], axis=0)
    g = dot(stacked(w), stacked_right(a))
    val = jnp.concatenate(
        [g[4 * k : 4 * k + 4, v * count : (v + 1) * count] for k in range(3) for v in range(2)], axis=0
    )
    spot = spot_ref[...].reshape(1, count)
    row, col = spot >> 10, spot & 1023
    below = jnp.where(row == 0, col + 1025, 0)
    above = jnp.where(row == 1, col + 1, 0)
    vals = jnp.concatenate(
        [val, (spot + 1).astype(F32), below.astype(F32), above.astype(F32), jnp.zeros((5, count), F32)],
        axis=0,
    )
    slots = split(
        jnp.concatenate([jnp.where(rank == r, vals, 0.0) for r in range(CAP)], axis=0)
    )
    msg = dot_rows(hot16, slots[0]) + dot_rows(hot16, slots[1])
    at, kind = iota(msg.shape, 0), iota(msg.shape, 1) % LANES
    up = jnp.where(at == tiles - 1, 0.0, pltpu.roll(msg, tiles - 1, 0))
    down = jnp.where(at == 0, 0.0, pltpu.roll(msg, 1, 0))
    msg_ref[:, 0, :] = jnp.where(kind == 25, up, jnp.where(kind == 26, down, msg))


CORNER = [(1, 1), (1, 2), (2, 1)]


def pack_kernel(x_ref, lo_ref, hi_ref, above_ref, below_ref, after_ref, up_ref, down_ref):
    for i, (k, d) in enumerate(CORNER):
        for j, (ref, l) in enumerate(((above_ref, 3 - k), (below_ref, k - 1))):
            up_ref[:, 3 * j + i] = ref[:, l, 2 - d]
            down_ref[:, 3 * j + i] = ref[:, l, d - 1]
    for l in range(4):
        up_ref[:, 6 + l] = x_ref[:, l, 0]
        down_ref[:, 6 + l] = x_ref[:, l, 1]
        up_ref[:, 10 + l] = lo_ref[:, l]
        down_ref[:, 10 + l] = hi_ref[:, l]


def top_kernel(x_ref, lo_ref, hi_ref, coup_ref, block_ref, top_ref, mix_ref):
    c = coup_ref[...]
    cb = jnp.dot(c, block_ref[...], precision=EXACT, preferred_element_type=F32)
    nt = (((1,), (1,)), ((), ()))
    mix_ref[0] = lax.dot_general(c, c, nt, precision=EXACT, preferred_element_type=F32)
    mix_ref[1] = lax.dot_general(cb, c, nt, precision=EXACT, preferred_element_type=F32)

    def s0(l, r):
        return lo_ref[:, l] if r < 0 else hi_ref[:, l] if r > 1 else x_ref[:, l, r]

    for r in range(2):
        rows = pl.ds(8 * r, 8)
        first = []
        for l in range(2):
            here = s0(l, r)
            s = here[:8]
            around = beside(s) + s0(l + 1, r)[:8] + s0(l, r - 1)[:8] + s0(l, r + 1)[:8]
            if l > 0:
                around = around + s0(l - 1, r)[:8]
            first.append(local_part(s, here[8:9], around))
        top_ref[0:8, rows, :] = first[0]
        top_ref[8:16, rows, :] = -2.0 * HOP * signed(first[1]) - s0(0, r)[:8]
        top_ref[16:25, rows, :] = s0(0, r)


def pure_kernel(
    pos_ref, x_ref, lo_ref, hi_ref, low2_ref, high2_ref, above_ref, below_ref, after_ref,
    one_ref, two_ref, s1_ref,
):
    first_layer = pos_ref[0] == 0
    last_layer = pos_ref[0] == pos_ref[1] - 1
    first_row = pos_ref[2] == 0
    last_row = pos_ref[2] == pos_ref[3] - 1

    def masked(s, l, r):
        out = None
        for cond, flag in (
            (l < 0, first_layer), (l > 3, last_layer), (r < 0, first_row), (r > 1, last_row)
        ):
            if cond:
                out = flag if out is None else out | flag
        return s if out is None else jnp.where(out, 0.0, s)

    def start(l, r):
        k, d = max(-l, l - 3), max(-r, r - 1)
        side = low2_ref if r < 0 else high2_ref
        if k > 0 and d > 0:
            return side[:, (0 if l < 0 else 3) + CORNER.index((k, d))]
        if k > 0:
            return above_ref[:, 3 - k, r] if l < 0 else below_ref[:, k - 1, r]
        if d > 1:
            return side[:, 4 * d - 2 + l]
        return lo_ref[:, l] if r < 0 else hi_ref[:, l] if r > 1 else x_ref[:, l, r]

    def s0(l, r):
        return start(l, r)[:8]

    def beyond(l, r):
        return max(-l, l - 3, 0) + max(-r, r - 1, 0)

    for l in range(-2, 6):
        for r in range(-2, 4):
            if beyond(l, r) > 2:
                continue
            here = start(l, r)
            s = here[:8]
            around = beside(s) + s0(l - 1, r) + s0(l + 1, r) + s0(l, r - 1) + s0(l, r + 1)
            s1_ref[:, l + 2, r + 2] = masked(local_part(s, here[8:9], around), l, r)
    for l in range(-1, 5):
        for r in range(-1, 3):
            if beyond(l, r) > 1:
                continue
            s = s1_ref[:, l + 2, r + 2]
            around = beside(s) + s1_ref[:, l + 1, r + 2] + s1_ref[:, l + 3, r + 2]
            around = around + s1_ref[:, l + 2, r + 1] + s1_ref[:, l + 2, r + 3]
            new = 2.0 * local_part(s, start(l, r)[8:9], around) - s0(l, r)
            two_ref[:, l + 1, r + 1] = masked(new, l, r)
            if beyond(l, r) == 0:
                one_ref[:, l, r] = s


def mix(k, s):
    def row(o):
        terms = [k[o : o + 1, q : q + 1] * s[2 * q : 2 * q + 2] for q in range(4)]
        return (terms[0] + terms[1]) + (terms[2] + terms[3])

    return jnp.concatenate([row(o) for o in range(4)], axis=0)


def columns(got):
    width = got.shape[1] // 128
    return jnp.concatenate([got[:, 128 * j : 128 * (j + 1)].T for j in range(width)], axis=0)


def scatter_kernel(pos_ref, got_ref, top_ref, mix_ref, out_ref, d2_ref, site_ref, dense_ref):
    got = got_ref[:, 0, :]
    tiles = got.shape[0]
    slots = columns(got)
    sub = iota((256, tiles), 0)
    total = None
    for r in range(CAP):
        vals = slots[r * LANES : r * LANES + 24]
        sites = slots[r * LANES + 24 : r * LANES + 27].astype(jnp.int32) - 1
        site_ref[r : r + 1] = sites[0:1]
        site_ref[16 + r : 17 + r] = sites[1:2]
        site_ref[32 + r : 33 + r] = sites[2:3]
        high = sites[0:1] >> 8
        near = vals.astype(BF16).astype(F32)
        number = (iota((8, tiles), 0) == high).astype(F32)
        left = jnp.concatenate(
            [
                jnp.concatenate([jnp.where(high == h, part, 0.0) for h in range(8)] + [last], axis=0)
                for part, last in ((near, number), (vals - near, jnp.zeros_like(number)))
            ],
            axis=1,
        ).astype(BF16)
        right = (sub == (sites[0:1] & 255)).astype(F32).astype(BF16)
        part = dot_rows(left, jnp.concatenate([right, right], axis=1))
        total = part if total is None else total + part
    dense_ref[0] = total[:, :128]
    dense_ref[1] = total[:, 128:]

    on = pos_ref[0] == 0
    for j in range(2):
        rows = pl.ds(j, 8, stride=2)

        def dense(k):
            k = k - k % 8 + (k % 2) * 4 + (k % 8) // 2
            return dense_ref[j, pl.ds(k, 8, stride=24), :]

        number = dense_ref[j, 192:200, :]
        d2_ref[8, rows, :] = number
        mixed = mix(mix_ref[0], top_ref[16:24, rows, :])
        for k in range(8):
            q1 = dense(k) + jnp.where(on, top_ref[k, rows, :], 0.0)
            q2 = top_ref[8 + k, rows, :] + 2.0 * (number * mixed[k])
            q2 = 2.0 * dense(8 + k) + jnp.where(on, q2, 0.0)
            d2 = dense(16 + k)
            d2_ref[k, rows, :] = d2
            tail = jnp.where(on, top_ref[16 + k, rows, :], d2)
            for y in range(4):
                out_ref[y, k, rows, :] = q1
                out_ref[y, 8 + k, rows, :] = q2
                out_ref[y, 16 + k, rows, :] = tail
        tail = jnp.where(on, top_ref[24, rows, :], number)
        for y in range(4):
            out_ref[y, 24, rows, :] = tail


def evolve_kernel(
    pos_ref, m_ref, top_ref, d2_ref, site_ref, mix_ref,
    ans_ref, d_ref, f_ref, f1_ref,
):
    tiles = site_ref.shape[1]
    on = pos_ref[0] == 0
    kk, kb = mix_ref[0], mix_ref[1]

    def rows_of(s):
        return s.reshape(s.shape[0], 2, 8, 128)

    s0 = m_ref[0, 16:24]
    field = rows_of(m_ref[0, 24:25])
    s1 = (m_ref[0, 0:8] + m_ref[1, 0:8]) + (m_ref[2, 0:8] + m_ref[3, 0:8])
    q2 = (m_ref[0, 8:16] + m_ref[1, 8:16]) + (m_ref[2, 8:16] + m_ref[3, 8:16])
    number = m_ref[1, 24:25] + m_ref[2, 24:25] + m_ref[3, 24:25]

    def flat_part(s):
        s = rows_of(s)
        other = jnp.concatenate([s[:, 1:2], s[:, 0:1]], axis=1)
        return local_part(s, field, beside(s) + other).reshape(8, 16, 128)

    hopped = q2 + 2.0 * (number * mix(kk, s0))
    s2 = hopped + 2.0 * flat_part(s1)
    d0 = jnp.where(on, s1 - top_ref[0:8], 0.0)
    delta = jnp.where(on, hopped - top_ref[8:16] + 2.0 * flat_part(d0), 0.0)
    number = number + d2_ref[8:9]
    d2 = d2_ref[0:8] + (m_ref[1, 16:24] + m_ref[2, 16:24] + m_ref[3, 16:24])
    third = 2.0 * (d2 + number * (mix(kb, s0) + mix(kk, s1))) - d0
    d_ref[0:8] = d0
    d_ref[8:16] = delta
    d_ref[16:24] = jnp.where(on, third, 0.0)
    for k in range(8):
        f_ref[pl.ds(k, 16, stride=24), :] = s0[k]
        f_ref[pl.ds(8 + k, 16, stride=24), :] = s1[k]
        f_ref[pl.ds(16 + k, 16, stride=24), :] = s2[k]
        f1_ref[pl.ds(k, 16, stride=8), :] = s1[k]
    f = jnp.concatenate(split(f_ref[...]), axis=1)
    f1 = jnp.concatenate(split(f1_ref[...]), axis=1)
    sub = iota((128, 2 * tiles), 0)

    def pick(table, width, sites):
        right = (sub == (sites & 127)).astype(F32).astype(BF16)
        found = dot(table, jnp.concatenate([right, right], axis=0))
        high = sites >> 7
        out = jnp.zeros((width, sites.shape[1]), F32)
        for h in range(16):
            out = out + jnp.where(high == h, found[h * width : (h + 1) * width], 0.0)
        return out

    own, low, high = [], [], []
    for r in range(0, CAP, 2):
        for table, width, base, out in ((f, 24, 0, own), (f1, 8, 16, low), (f1, 8, 32, high)):
            sites = jnp.concatenate(
                [site_ref[base + r : base + r + 1], site_ref[base + r + 1 : base + r + 2]], axis=1
            )
            both = pick(table, width, sites)
            out += [both[:, :tiles], both[:, tiles:]]
    answer = jnp.concatenate(own + low + high + [jnp.zeros((32, tiles), F32)], axis=0)
    for j in range(4):
        ans_ref[:, j, :] = answer[128 * j : 128 * (j + 1)].T


def adatom_kernel(a_ref, back_ref, tile_ref, rank_ref, block_ref, coup_ref, prev_ref, last_ref):
    count = a_ref.shape[2]
    tiles = back_ref.shape[0]
    back = jnp.concatenate([back_ref[:, j, :].T for j in range(4)], axis=0)
    back = jnp.concatenate(
        [back[:288], pltpu.roll(back[288:384], 1, 1), pltpu.roll(back[384:480], tiles - 1, 1)], axis=0
    )
    hot = (iota((tiles, count), 0) == tile_ref[...]).astype(F32).astype(BF16)
    found = dot(jnp.concatenate(split(back), axis=1), jnp.concatenate([hot, hot], axis=0))
    rank = rank_ref[...]
    s = jnp.zeros((24, count), F32)
    halo = jnp.zeros((8, count), F32)
    for r in range(CAP):
        here = rank == r
        s = s + jnp.where(here, found[24 * r : 24 * r + 24], 0.0)
        near = found[288 + 8 * r : 296 + 8 * r] + found[384 + 8 * r : 392 + 8 * r]
        halo = halo + jnp.where(here, near, 0.0)
    sign = jnp.where(iota((8, count), 0) < 4, 1.0, -1.0)
    s2 = s[16:24] - 2.0 * HOP * sign * halo
    i, j = iota((4, 8), 0), iota((4, 8), 1)
    spread = (i == j // 2).astype(F32)
    c = lax.dot_general(
        coup_ref[...], spread, (((0,), (0,)), ((), ())), precision=EXACT, preferred_element_type=F32
    )
    w = stacked(jnp.concatenate([block_ref[...], c], axis=1))
    even = iota((8, count), 0) % 2 == 0

    def apply(a, s):
        s = jnp.concatenate([jnp.where(even, s, 0.0), jnp.where(even, 0.0, s)], axis=1)
        return dot(w, stacked_right(jnp.concatenate([a, s], axis=0)))

    a0 = jnp.concatenate([a_ref[:, 0, :], a_ref[:, 1, :]], axis=1)
    a1 = apply(a0, s[0:8])
    a2 = 2.0 * apply(a1, s[8:16]) - a0
    a3 = 2.0 * apply(a2, s2) - a1
    for v in range(2):
        prev_ref[:, v, :] = a2[:, v * count : (v + 1) * count]
        last_ref[:, v, :] = a3[:, v * count : (v + 1) * count]


def last_kernel(pos_ref, x_ref, one_ref, two_ref, d_ref, before_ref, after_ref, prev_ref, last_ref):
    has_before = pos_ref[2] > 0
    has_after = pos_ref[2] < pos_ref[3] - 1
    d0 = d_ref[0:8].reshape(8, 2, 8, 128)
    delta = d_ref[8:16].reshape(8, 2, 8, 128)
    third = d_ref[16:24].reshape(8, 2, 8, 128)

    def hop(s):
        return -2.0 * HOP * signed(s)

    hop0 = [hop(d0[:, r]) for r in range(2)]
    for r, ref in ((0, before_ref), (1, after_ref)):
        prev_ref[:, 0, r] = two_ref[:, 1, r + 1] + delta[:, r] + hop(ref[0:8])
        prev_ref[:, 1, r] = two_ref[:, 2, r + 1] + hop0[r]
        prev_ref[:, 2, r] = two_ref[:, 3, r + 1]
        prev_ref[:, 3, r] = two_ref[:, 4, r + 1]

    def beyond(l, r):
        ref, there = (before_ref, has_before) if r == 0 else (after_ref, has_after)
        s = two_ref[:, l + 1, 3 * r]
        if l == 0:
            s = s + ref[8:16] + jnp.where(there, hop0[r], 0.0)
        if l == 1:
            s = s + hop(ref[0:8])
        return s

    for l in range(4):
        for r in range(2):
            s = prev_ref[:, l, r]
            over = two_ref[:, 0, r + 1] if l == 0 else prev_ref[:, l - 1, r]
            under = two_ref[:, 5, r + 1] if l == 3 else prev_ref[:, l + 1, r]
            around = beside(s) + over + under + prev_ref[:, l, 1 - r] + beyond(l, r)
            new = 2.0 * local_part(s, x_ref[8:9, l, r], around) - one_ref[:, l, r]
            if l == 0:
                new = new + 2.0 * third[:, r] - d0[:, r]
            last_ref[:, l, r] = new


VM = pl.BlockSpec(memory_space=pltpu.VMEM)
SM = pl.BlockSpec(memory_space=pltpu.SMEM)


def shape(*dims, dtype=F32):
    return jax.ShapeDtypeStruct(dims, dtype)


def call(kernel, name, outs, args, scratch=(), smem=False, cost=0, space=pltpu.VMEM, limit=16):
    return pl.pallas_call(
        kernel,
        out_shape=outs,
        in_specs=[SM if smem and i == 0 else pl.BlockSpec(memory_space=space) for i in range(len(args))],
        out_specs=[VM] * len(outs),
        scratch_shapes=list(scratch),
        name=name,
        cost_estimate=pl.CostEstimate(flops=cost, bytes_accessed=0, transcendentals=0),
        compiler_params=pltpu.CompilerParams(vmem_limit_bytes=limit * 2**20),
    )(*args)


def per_device(
    substrate_start, adatom_start, disorder, adatom_block, coupling, adatom_tile, adatom_spot
):
    tiles, depths = lax.axis_size("tile"), lax.axis_size("depth")
    t, y = lax.axis_index("tile"), lax.axis_index("depth")
    count = adatom_spot.shape[0]
    pos = jnp.stack([y, jnp.int32(depths), t, jnp.int32(tiles)])

    def shifted(x, axis, size, step):
        pairs = [(i, i + step) for i in range(size) if 0 <= i + step < size]
        return lax.ppermute(x, axis, pairs)

    own_tile = adatom_tile.reshape(1, count)
    msg, rank = call(
        route_kernel, "route",
        (shape(tiles, 1, CAP * LANES), shape(1, count, dtype=jnp.int32)),
        (adatom_start, own_tile, adatom_spot, adatom_block, coupling),
        (
            pltpu.VMEM((40, 2, count), F32), pltpu.VMEM((1, count), jnp.int32), pltpu.VMEM((count,), jnp.int32),
            pltpu.VMEM((40, 40), F32), pltpu.VMEM((4, 40), F32), pltpu.SemaphoreType.DMA((5,)),
        ),
        space=pl.ANY, limit=60
    )
    substrate, disorder, rank = lax.optimization_barrier((substrate_start, disorder, rank))
    got = lax.all_to_all(msg, "tile", split_axis=0, concat_axis=0, tiled=True)
    x = jnp.concatenate(
        [substrate.reshape(8, 4, 2, 8, 128), disorder.reshape(1, 4, 2, 8, 128)], axis=0
    )
    lo = shifted(x[:, :, 1], "tile", tiles, 1)
    hi = shifted(x[:, :, 0], "tile", tiles, -1)
    above = shifted(x[:, 1:], "depth", depths, 1)
    below = shifted(x[:, :3], "depth", depths, -1)
    top, mix_products = call(
        top_kernel, "top", (shape(25, 16, 128), shape(2, 4, 4)), (x, lo, hi, coupling, adatom_block),
        cost=2*10**9,
    )
    part, d2, site = call(
        scatter_kernel, "scatter",
        (shape(4, 25, 16, 128), shape(9, 16, 128), shape(48, tiles, dtype=jnp.int32)),
        (pos, got, top, mix_products),
        (pltpu.VMEM((2, 200, 128), F32),), smem=True,
    )
    up, down = call(
        pack_kernel, "pack", (shape(9, 14, 8, 128), shape(9, 14, 8, 128)), (x, lo, hi, above, below, site),
        cost=10**10,
    )
    low2 = shifted(up, "tile", tiles, 1)
    high2 = shifted(down, "tile", tiles, -1)
    part = lax.all_to_all(part, "depth", split_axis=0, concat_axis=0, tiled=True)
    answer, d = call(
        evolve_kernel, "evolve",
        (shape(tiles, 4, 128), shape(24, 16, 128)),
        (pos, part, top, d2, site, mix_products),
        (pltpu.VMEM((384, 128), F32), pltpu.VMEM((128, 128), F32)), smem=True,
    )
    before = shifted(d[:16, 8:], "tile", tiles, 1)
    after = shifted(d[:16, :8], "tile", tiles, -1)
    one, two = call(
        pure_kernel, "pure",
        (shape(8, 4, 2, 8, 128), shape(8, 6, 4, 8, 128)),
        (pos, x, lo, hi, low2, high2, above, below, d),
        (pltpu.VMEM((8, 8, 6, 8, 128), F32),), smem=True, cost=10**10,
    )
    back = lax.all_to_all(answer, "tile", split_axis=0, concat_axis=0, tiled=True)
    sub_prev, sub_last = call(
        last_kernel, "last",
        (shape(8, 4, 2, 8, 128), shape(8, 4, 2, 8, 128)),
        (pos, x, one, two, d, before, after), smem=True,
    )
    ad_prev, ad_last = call(
        adatom_kernel, "adatoms",
        (shape(40, 2, count), shape(40, 2, count)),
        (adatom_start, back, own_tile, rank, adatom_block, coupling),
    )
    return (
        sub_prev.reshape(4, 2, 4, 2, 1024),
        sub_last.reshape(4, 2, 4, 2, 1024),
        ad_prev,
        ad_last,
    )


def solution(mesh):
    in_specs = (
        P(None, None, "depth", "tile", None),
        P(None, None, ("tile", "depth")),
        P("depth", "tile", None),
        P(),
        P(),
        P(("tile", "depth"), None),
        P(("tile", "depth")),
    )
    out_specs = (
        P(None, None, "depth", "tile", None),
        P(None, None, "depth", "tile", None),
        P(None, None, ("tile", "depth")),
        P(None, None, ("tile", "depth")),
    )
    return jax.shard_map(
        per_device, mesh=mesh, in_specs=in_specs, out_specs=out_specs, check_vma=False
    )
```

```python
import jax
import jax.numpy as jnp
from jax import lax
from jax.experimental import pallas as pl
from jax.experimental.pallas import tpu as pltpu
from jax.sharding import PartitionSpec as P

HOP = 0.12
MU = 0.15
PAIR = 0.3
CAP = 12
LANES = 32
EXACT = lax.Precision.HIGHEST
F32 = jnp.float32
BF16 = jnp.bfloat16


def iota(shape, dim):
    return lax.broadcasted_iota(jnp.int32, shape, dim)


def split(x):
    high = x.astype(BF16)
    return high, (x - high.astype(F32)).astype(BF16)


def dot(a, b):
    return jnp.dot(a, b, preferred_element_type=F32)


def dot3(a, b):
    return dot(a[0], b[0]) + dot(a[0], b[1]) + dot(a[1], b[0])


def dot_rows(a, b):
    return lax.dot_general(a, b, (((1,), (1,)), ((), ())), preferred_element_type=F32)


def beside(s):
    rank = s.ndim
    sub, lane = iota(s.shape, rank - 2), iota(s.shape, rank - 1)
    left = pltpu.roll(s, 1, rank - 1)
    left = jnp.where(lane == 0, pltpu.roll(left, 1, rank - 2), left)
    left = jnp.where((lane == 0) & (sub == 0), 0.0, left)
    right = pltpu.roll(s, 127, rank - 1)
    right = jnp.where(lane == 127, pltpu.roll(right, 7, rank - 2), right)
    right = jnp.where((lane == 127) & (sub == 7), 0.0, right)
    return left + right


def local_part(s, disorder, around):
    inner = (disorder - MU) * s - HOP * around
    return jnp.concatenate(
        [inner[:4] + PAIR * s[4:], PAIR * s[:4] - inner[4:]], axis=0
    )


def signed(s):
    return jnp.concatenate([s[:4], -s[4:]], axis=0)


def stacked(w):
    high, low = split(w)
    return jnp.concatenate([high, low, high], axis=1)


def stacked_right(x):
    high, low = split(x)
    return jnp.concatenate([high, high, low], axis=0)


def route_kernel(
    a_hbm, tile_hbm, spot_hbm, block_hbm, coup_hbm, msg_ref, rank_ref,
    a_ref, tile_ref, spot_ref, block_ref, coup_ref, sems,
):
    pairs = (
        (tile_hbm, tile_ref), (spot_hbm, spot_ref), (block_hbm, block_ref), (coup_hbm, coup_ref), (a_hbm, a_ref)
    )
    copies = [pltpu.make_async_copy(src, dst, sems.at[i]) for i, (src, dst) in enumerate(pairs)]
    for copy in copies:
        copy.start()
    count = a_ref.shape[2]
    tiles = msg_ref.shape[0]
    part = 256
    earlier = (iota((part, part), 0) < iota((part, part), 1)).astype(F32).astype(BF16)
    for copy in copies[:4]:
        copy.wait()
    c, b = coup_ref[...], block_ref[...]
    cb = jnp.dot(c, b, precision=EXACT, preferred_element_type=F32)
    cbb = jnp.dot(cb, b, precision=EXACT, preferred_element_type=F32)
    hot = (iota((tiles, count), 0) == tile_ref[...]).astype(F32)
    hot16 = hot.astype(BF16)
    ranks, seen = [], jnp.zeros((tiles, 1), F32)
    for k in range(0, count, part):
        chunk = hot[:, k : k + part]
        ranks.append(jnp.sum((dot(hot16[:, k : k + part], earlier) + seen) * chunk, axis=0, keepdims=True))
        seen = seen + jnp.sum(chunk, axis=1, keepdims=True)
    rank = jnp.concatenate(ranks, axis=1).astype(jnp.int32)
    rank_ref[...] = rank
    copies[4].wait()
    a = jnp.concatenate([a_ref[:, 0, :], a_ref[:, 1, :]], axis=1)
    pad = jnp.zeros((12, 8), F32)
    w = jnp.concatenate([jnp.concatenate([c, cb, cbb], axis=0), pad], axis=1)
    a = jnp.concatenate([a, jnp.zeros((8, 2 * count), F32)], axis=0)
    g = dot(stacked(w), stacked_right(a))
    val = jnp.concatenate(
        [g[4 * k : 4 * k + 4, v * count : (v + 1) * count] for k in range(3) for v in range(2)], axis=0
    )
    spot = spot_ref[...].reshape(1, count)
    row, col = spot >> 10, spot & 1023
    below = jnp.where(row == 0, col + 1025, 0)
    above = jnp.where(row == 1, col + 1, 0)
    vals = jnp.concatenate(
        [val, (spot + 1).astype(F32), below.astype(F32), above.astype(F32), jnp.zeros((5, count), F32)],
        axis=0,
    )
    slots = split(
        jnp.concatenate([jnp.where(rank == r, vals, 0.0) for r in range(CAP)], axis=0)
    )
    msg = dot_rows(hot16, slots[0]) + dot_rows(hot16, slots[1])
    at, kind = iota(msg.shape, 0), iota(msg.shape, 1) % LANES
    up = jnp.where(at == tiles - 1, 0.0, pltpu.roll(msg, tiles - 1, 0))
    down = jnp.where(at == 0, 0.0, pltpu.roll(msg, 1, 0))
    msg_ref[:, 0, :] = jnp.where(kind == 25, up, jnp.where(kind == 26, down, msg))


CORNER = [(1, 1), (1, 2), (2, 1)]


def pack_kernel(x_ref, lo_ref, hi_ref, above_ref, below_ref, after_ref, up_ref, down_ref):
    for i, (k, d) in enumerate(CORNER):
        for j, (ref, l) in enumerate(((above_ref, 3 - k), (below_ref, k - 1))):
            up_ref[:, 3 * j + i] = ref[:, l, 2 - d]
            down_ref[:, 3 * j + i] = ref[:, l, d - 1]
    for l in range(4):
        up_ref[:, 6 + l] = x_ref[:, l, 0]
        down_ref[:, 6 + l] = x_ref[:, l, 1]
        up_ref[0:8, 10 + l] = lo_ref[:, l]
        down_ref[0:8, 10 + l] = hi_ref[:, l]
        up_ref[8:9, 10 + l] = x_ref[8:9, l, 1]
        down_ref[8:9, 10 + l] = x_ref[8:9, l, 0]


def top_kernel(x_ref, lo_ref, hi_ref, coup_ref, block_ref, top_ref, mix_ref):
    c = coup_ref[...]
    cb = jnp.dot(c, block_ref[...], precision=EXACT, preferred_element_type=F32)
    nt = (((1,), (1,)), ((), ()))
    mix_ref[0] = lax.dot_general(c, c, nt, precision=EXACT, preferred_element_type=F32)
    mix_ref[1] = lax.dot_general(cb, c, nt, precision=EXACT, preferred_element_type=F32)

    def s0(l, r):
        return lo_ref[:, l] if r < 0 else hi_ref[:, l] if r > 1 else x_ref[:, l, r]

    for r in range(2):
        rows = pl.ds(8 * r, 8)
        first = []
        for l in range(2):
            here = s0(l, r)
            s = here[:8]
            around = beside(s) + s0(l + 1, r)[:8] + s0(l, r - 1)[:8] + s0(l, r + 1)[:8]
            if l > 0:
                around = around + s0(l - 1, r)[:8]
            first.append(local_part(s, here[8:9], around))
        top_ref[0:8, rows, :] = first[0]
        top_ref[8:16, rows, :] = -2.0 * HOP * signed(first[1]) - s0(0, r)[:8]
        top_ref[16:25, rows, :] = s0(0, r)


def pure_kernel(
    pos_ref, x_ref, lo_ref, hi_ref, low2_ref, high2_ref, above_ref, below_ref, after_ref,
    one_ref, two_ref, s1_ref,
):
    first_layer = pos_ref[0] == 0
    last_layer = pos_ref[0] == pos_ref[1] - 1
    first_row = pos_ref[2] == 0
    last_row = pos_ref[2] == pos_ref[3] - 1

    def masked(s, l, r):
        out = None
        for cond, flag in (
            (l < 0, first_layer), (l > 3, last_layer), (r < 0, first_row), (r > 1, last_row)
        ):
            if cond:
                out = flag if out is None else out | flag
        return s if out is None else jnp.where(out, 0.0, s)

    def start(l, r):
        k, d = max(-l, l - 3), max(-r, r - 1)
        side = low2_ref if r < 0 else high2_ref
        if k > 0 and d > 0:
            return side[:, (0 if l < 0 else 3) + CORNER.index((k, d))]
        if k > 0:
            return above_ref[:, 3 - k, r] if l < 0 else below_ref[:, k - 1, r]
        if d > 1:
            return side[:, 4 * d - 2 + l]
        return lo_ref[:, l] if r < 0 else hi_ref[:, l] if r > 1 else x_ref[:, l, r]

    def s0(l, r):
        return start(l, r)[:8]

    def potential(l, r):
        if 0 <= l < 4 and r in (-1, 2):
            return (low2_ref if r < 0 else high2_ref)[8:9, 10 + l]
        return start(l, r)[8:9]

    def beyond(l, r):
        return max(-l, l - 3, 0) + max(-r, r - 1, 0)

    for l in range(-2, 6):
        for r in range(-2, 4):
            if beyond(l, r) > 2:
                continue
            s = s0(l, r)
            around = beside(s) + s0(l - 1, r) + s0(l + 1, r) + s0(l, r - 1) + s0(l, r + 1)
            s1_ref[:, l + 2, r + 2] = masked(local_part(s, potential(l, r), around), l, r)
    for l in range(-1, 5):
        for r in range(-1, 3):
            if beyond(l, r) > 1:
                continue
            s = s1_ref[:, l + 2, r + 2]
            around = beside(s) + s1_ref[:, l + 1, r + 2] + s1_ref[:, l + 3, r + 2]
            around = around + s1_ref[:, l + 2, r + 1] + s1_ref[:, l + 2, r + 3]
            new = 2.0 * local_part(s, potential(l, r), around) - s0(l, r)
            two_ref[:, l + 1, r + 1] = masked(new, l, r)
            if beyond(l, r) == 0:
                one_ref[:, l, r] = s


def mix(k, s):
    def row(o):
        terms = [k[o : o + 1, q : q + 1] * s[2 * q : 2 * q + 2] for q in range(4)]
        return (terms[0] + terms[1]) + (terms[2] + terms[3])

    return jnp.concatenate([row(o) for o in range(4)], axis=0)


def columns(got):
    width = got.shape[1] // 128
    return jnp.concatenate([got[:, 128 * j : 128 * (j + 1)].T for j in range(width)], axis=0)


def scatter_kernel(pos_ref, got_ref, top_ref, mix_ref, out_ref, d2_ref, site_ref, dense_ref):
    got = got_ref[:, 0, :]
    tiles = got.shape[0]
    slots = columns(got)
    sub = iota((256, tiles), 0)
    total = None
    for r in range(CAP):
        vals = slots[r * LANES : r * LANES + 24]
        sites = slots[r * LANES + 24 : r * LANES + 27].astype(jnp.int32) - 1
        site_ref[r : r + 1] = sites[0:1]
        site_ref[16 + r : 17 + r] = sites[1:2]
        site_ref[32 + r : 33 + r] = sites[2:3]
        high = sites[0:1] >> 8
        near = vals.astype(BF16).astype(F32)
        number = (iota((8, tiles), 0) == high).astype(F32)
        left = jnp.concatenate(
            [
                jnp.concatenate([jnp.where(high == h, part, 0.0) for h in range(8)] + [last], axis=0)
                for part, last in ((near, number), (vals - near, jnp.zeros_like(number)))
            ],
            axis=1,
        ).astype(BF16)
        right = (sub == (sites[0:1] & 255)).astype(F32).astype(BF16)
        part = dot_rows(left, jnp.concatenate([right, right], axis=1))
        total = part if total is None else total + part
    dense_ref[0] = total[:, :128]
    dense_ref[1] = total[:, 128:]

    on = pos_ref[0] == 0
    for j in range(2):
        rows = pl.ds(j, 8, stride=2)

        def dense(k):
            k = k - k % 8 + (k % 2) * 4 + (k % 8) // 2
            return dense_ref[j, pl.ds(k, 8, stride=24), :]

        number = dense_ref[j, 192:200, :]
        d2_ref[8, rows, :] = number
        mixed = mix(mix_ref[0], top_ref[16:24, rows, :])
        for k in range(8):
            q1 = dense(k) + jnp.where(on, top_ref[k, rows, :], 0.0)
            q2 = top_ref[8 + k, rows, :] + 2.0 * (number * mixed[k])
            q2 = 2.0 * dense(8 + k) + jnp.where(on, q2, 0.0)
            d2 = dense(16 + k)
            d2_ref[k, rows, :] = d2
            tail = jnp.where(on, top_ref[16 + k, rows, :], d2)
            for y in range(4):
                out_ref[y, k, rows, :] = q1
                out_ref[y, 8 + k, rows, :] = q2
                out_ref[y, 16 + k, rows, :] = tail
        tail = jnp.where(on, top_ref[24, rows, :], number)
        for y in range(4):
            out_ref[y, 24, rows, :] = tail


def evolve_kernel(
    pos_ref, m_ref, top_ref, d2_ref, site_ref, mix_ref,
    ans_ref, d_ref, f_ref, f1_ref,
):
    tiles = site_ref.shape[1]
    on = pos_ref[0] == 0
    kk, kb = mix_ref[0], mix_ref[1]

    def rows_of(s):
        return s.reshape(s.shape[0], 2, 8, 128)

    s0 = m_ref[0, 16:24]
    field = rows_of(m_ref[0, 24:25])
    s1 = (m_ref[0, 0:8] + m_ref[1, 0:8]) + (m_ref[2, 0:8] + m_ref[3, 0:8])
    q2 = (m_ref[0, 8:16] + m_ref[1, 8:16]) + (m_ref[2, 8:16] + m_ref[3, 8:16])
    number = m_ref[1, 24:25] + m_ref[2, 24:25] + m_ref[3, 24:25]

    def flat_part(s):
        s = rows_of(s)
        other = jnp.concatenate([s[:, 1:2], s[:, 0:1]], axis=1)
        return local_part(s, field, beside(s) + other).reshape(8, 16, 128)

    hopped = q2 + 2.0 * (number * mix(kk, s0))
    s2 = hopped + 2.0 * flat_part(s1)
    d0 = jnp.where(on, s1 - top_ref[0:8], 0.0)
    delta = jnp.where(on, hopped - top_ref[8:16] + 2.0 * flat_part(d0), 0.0)
    number = number + d2_ref[8:9]
    d2 = d2_ref[0:8] + (m_ref[1, 16:24] + m_ref[2, 16:24] + m_ref[3, 16:24])
    third = 2.0 * (d2 + number * (mix(kb, s0) + mix(kk, s1))) - d0
    d_ref[0:8] = d0
    d_ref[8:16] = delta
    d_ref[16:24] = jnp.where(on, third, 0.0)
    for k in range(8):
        f_ref[pl.ds(k, 16, stride=24), :] = s0[k]
        f_ref[pl.ds(8 + k, 16, stride=24), :] = s1[k]
        f_ref[pl.ds(16 + k, 16, stride=24), :] = s2[k]
        f1_ref[pl.ds(k, 16, stride=8), :] = s1[k]
    f = jnp.concatenate(split(f_ref[...]), axis=1)
    f1 = jnp.concatenate(split(f1_ref[...]), axis=1)
    sub = iota((128, 2 * tiles), 0)

    def pick(table, width, sites):
        right = (sub == (sites & 127)).astype(F32).astype(BF16)
        found = dot(table, jnp.concatenate([right, right], axis=0))
        high = sites >> 7
        out = jnp.zeros((width, sites.shape[1]), F32)
        for h in range(16):
            out = out + jnp.where(high == h, found[h * width : (h + 1) * width], 0.0)
        return out

    own, low, high = [], [], []
    for r in range(0, CAP, 2):
        for table, width, base, out in ((f, 24, 0, own), (f1, 8, 16, low), (f1, 8, 32, high)):
            sites = jnp.concatenate(
                [site_ref[base + r : base + r + 1], site_ref[base + r + 1 : base + r + 2]], axis=1
            )
            both = pick(table, width, sites)
            out += [both[:, :tiles], both[:, tiles:]]
    answer = jnp.concatenate(own + low + high + [jnp.zeros((32, tiles), F32)], axis=0)
    for j in range(4):
        ans_ref[:, j, :] = answer[128 * j : 128 * (j + 1)].T


def adatom_kernel(a_ref, back_ref, tile_ref, rank_ref, block_ref, coup_ref, prev_ref, last_ref):
    count = a_ref.shape[2]
    tiles = back_ref.shape[0]
    back = jnp.concatenate([back_ref[:, j, :].T for j in range(4)], axis=0)
    back = jnp.concatenate(
        [back[:288], pltpu.roll(back[288:384], 1, 1), pltpu.roll(back[384:480], tiles - 1, 1)], axis=0
    )
    hot = (iota((tiles, count), 0) == tile_ref[...]).astype(F32).astype(BF16)
    found = dot(jnp.concatenate(split(back), axis=1), jnp.concatenate([hot, hot], axis=0))
    rank = rank_ref[...]
    s = jnp.zeros((24, count), F32)
    halo = jnp.zeros((8, count), F32)
    for r in range(CAP):
        here = rank == r
        s = s + jnp.where(here, found[24 * r : 24 * r + 24], 0.0)
        near = found[288 + 8 * r : 296 + 8 * r] + found[384 + 8 * r : 392 + 8 * r]
        halo = halo + jnp.where(here, near, 0.0)
    sign = jnp.where(iota((8, count), 0) < 4, 1.0, -1.0)
    s2 = s[16:24] - 2.0 * HOP * sign * halo
    i, j = iota((4, 8), 0), iota((4, 8), 1)
    spread = (i == j // 2).astype(F32)
    c = lax.dot_general(
        coup_ref[...], spread, (((0,), (0,)), ((), ())), precision=EXACT, preferred_element_type=F32
    )
    w = stacked(jnp.concatenate([block_ref[...], c], axis=1))
    even = iota((8, count), 0) % 2 == 0

    def apply(a, s):
        s = jnp.concatenate([jnp.where(even, s, 0.0), jnp.where(even, 0.0, s)], axis=1)
        return dot(w, stacked_right(jnp.concatenate([a, s], axis=0)))

    a0 = jnp.concatenate([a_ref[:, 0, :], a_ref[:, 1, :]], axis=1)
    a1 = apply(a0, s[0:8])
    a2 = 2.0 * apply(a1, s[8:16]) - a0
    a3 = 2.0 * apply(a2, s2) - a1
    for v in range(2):
        prev_ref[:, v, :] = a2[:, v * count : (v + 1) * count]
        last_ref[:, v, :] = a3[:, v * count : (v + 1) * count]


def last_kernel(pos_ref, x_ref, one_ref, two_ref, d_ref, before_ref, after_ref, prev_ref, last_ref):
    has_before = pos_ref[2] > 0
    has_after = pos_ref[2] < pos_ref[3] - 1
    d0 = d_ref[0:8].reshape(8, 2, 8, 128)
    delta = d_ref[8:16].reshape(8, 2, 8, 128)
    third = d_ref[16:24].reshape(8, 2, 8, 128)

    def hop(s):
        return -2.0 * HOP * signed(s)

    hop0 = [hop(d0[:, r]) for r in range(2)]
    for r, ref in ((0, before_ref), (1, after_ref)):
        prev_ref[:, 0, r] = two_ref[:, 1, r + 1] + delta[:, r] + hop(ref[0:8])
        prev_ref[:, 1, r] = two_ref[:, 2, r + 1] + hop0[r]
        prev_ref[:, 2, r] = two_ref[:, 3, r + 1]
        prev_ref[:, 3, r] = two_ref[:, 4, r + 1]

    def beyond(l, r):
        ref, there = (before_ref, has_before) if r == 0 else (after_ref, has_after)
        s = two_ref[:, l + 1, 3 * r]
        if l == 0:
            s = s + ref[8:16] + jnp.where(there, hop0[r], 0.0)
        if l == 1:
            s = s + hop(ref[0:8])
        return s

    for l in range(4):
        for r in range(2):
            s = prev_ref[:, l, r]
            over = two_ref[:, 0, r + 1] if l == 0 else prev_ref[:, l - 1, r]
            under = two_ref[:, 5, r + 1] if l == 3 else prev_ref[:, l + 1, r]
            around = beside(s) + over + under + prev_ref[:, l, 1 - r] + beyond(l, r)
            new = 2.0 * local_part(s, x_ref[8:9, l, r], around) - one_ref[:, l, r]
            if l == 0:
                new = new + 2.0 * third[:, r] - d0[:, r]
            last_ref[:, l, r] = new


VM = pl.BlockSpec(memory_space=pltpu.VMEM)
SM = pl.BlockSpec(memory_space=pltpu.SMEM)


def shape(*dims, dtype=F32):
    return jax.ShapeDtypeStruct(dims, dtype)


def call(kernel, name, outs, args, scratch=(), smem=False, cost=0, space=pltpu.VMEM, limit=16):
    return pl.pallas_call(
        kernel,
        out_shape=outs,
        in_specs=[SM if smem and i == 0 else pl.BlockSpec(memory_space=space) for i in range(len(args))],
        out_specs=[VM] * len(outs),
        scratch_shapes=list(scratch),
        name=name,
        cost_estimate=pl.CostEstimate(flops=cost, bytes_accessed=0, transcendentals=0),
        compiler_params=pltpu.CompilerParams(vmem_limit_bytes=limit * 2**20),
    )(*args)


def per_device(
    substrate_start, adatom_start, disorder, adatom_block, coupling, adatom_tile, adatom_spot
):
    tiles, depths = lax.axis_size("tile"), lax.axis_size("depth")
    t, y = lax.axis_index("tile"), lax.axis_index("depth")
    count = adatom_spot.shape[0]
    pos = jnp.stack([y, jnp.int32(depths), t, jnp.int32(tiles)])

    def shifted(x, axis, size, step):
        pairs = [(i, i + step) for i in range(size) if 0 <= i + step < size]
        return lax.ppermute(x, axis, pairs)

    own_tile = adatom_tile.reshape(1, count)
    msg, rank = call(
        route_kernel, "route",
        (shape(tiles, 1, CAP * LANES), shape(1, count, dtype=jnp.int32)),
        (adatom_start, own_tile, adatom_spot, adatom_block, coupling),
        (
            pltpu.VMEM((40, 2, count), F32), pltpu.VMEM((1, count), jnp.int32), pltpu.VMEM((count,), jnp.int32),
            pltpu.VMEM((40, 40), F32), pltpu.VMEM((4, 40), F32), pltpu.SemaphoreType.DMA((5,)),
        ),
        space=pl.ANY, limit=60
    )
    substrate, disorder, rank = lax.optimization_barrier((substrate_start, disorder, rank))
    got = lax.all_to_all(msg, "tile", split_axis=0, concat_axis=0, tiled=True)
    substrate = substrate.reshape(8, 4, 2, 8, 128)
    lo = shifted(substrate[:, :, 1], "tile", tiles, 1)
    hi = shifted(substrate[:, :, 0], "tile", tiles, -1)
    x = jnp.concatenate([substrate, disorder.reshape(1, 4, 2, 8, 128)], axis=0)
    above = shifted(x[:, 1:], "depth", depths, 1)
    below = shifted(x[:, :3], "depth", depths, -1)
    top, mix_products = call(
        top_kernel, "top", (shape(25, 16, 128), shape(2, 4, 4)), (x, lo, hi, coupling, adatom_block),
        cost=2*10**9,
    )
    part, d2, site = call(
        scatter_kernel, "scatter",
        (shape(4, 25, 16, 128), shape(9, 16, 128), shape(48, tiles, dtype=jnp.int32)),
        (pos, got, top, mix_products),
        (pltpu.VMEM((2, 200, 128), F32),), smem=True,
    )
    up, down = call(
        pack_kernel, "pack", (shape(9, 14, 8, 128), shape(9, 14, 8, 128)), (x, lo, hi, above, below, site),
        cost=10**10,
    )
    low2 = shifted(up, "tile", tiles, 1)
    high2 = shifted(down, "tile", tiles, -1)
    part = lax.all_to_all(part, "depth", split_axis=0, concat_axis=0, tiled=True)
    answer, d = call(
        evolve_kernel, "evolve",
        (shape(tiles, 4, 128), shape(24, 16, 128)),
        (pos, part, top, d2, site, mix_products),
        (pltpu.VMEM((384, 128), F32), pltpu.VMEM((128, 128), F32)), smem=True,
    )
    before = shifted(d[:16, 8:], "tile", tiles, 1)
    after = shifted(d[:16, :8], "tile", tiles, -1)
    one, two = call(
        pure_kernel, "pure",
        (shape(8, 4, 2, 8, 128), shape(8, 6, 4, 8, 128)),
        (pos, x, lo, hi, low2, high2, above, below, d),
        (pltpu.VMEM((8, 8, 6, 8, 128), F32),), smem=True, cost=10**10,
    )
    back = lax.all_to_all(answer, "tile", split_axis=0, concat_axis=0, tiled=True)
    sub_prev, sub_last = call(
        last_kernel, "last",
        (shape(8, 4, 2, 8, 128), shape(8, 4, 2, 8, 128)),
        (pos, x, one, two, d, before, after), smem=True,
    )
    ad_prev, ad_last = call(
        adatom_kernel, "adatoms",
        (shape(40, 2, count), shape(40, 2, count)),
        (adatom_start, back, own_tile, rank, adatom_block, coupling),
    )
    return (
        sub_prev.reshape(4, 2, 4, 2, 1024),
        sub_last.reshape(4, 2, 4, 2, 1024),
        ad_prev,
        ad_last,
    )


def solution(mesh):
    in_specs = (
        P(None, None, "depth", "tile", None),
        P(None, None, ("tile", "depth")),
        P("depth", "tile", None),
        P(),
        P(),
        P(("tile", "depth"), None),
        P(("tile", "depth")),
    )
    out_specs = (
        P(None, None, "depth", "tile", None),
        P(None, None, "depth", "tile", None),
        P(None, None, ("tile", "depth")),
        P(None, None, ("tile", "depth")),
    )
    return jax.shard_map(
        per_device, mesh=mesh, in_specs=in_specs, out_specs=out_specs, check_vma=False
    )
```
